512 devices in a mesh: wide: 64 (over x, z), narrow: 8 (over y, core).
Axes of the slice: x: 4, y: 4, z: 16, core: 2. Of those that a mesh axis runs over, the one named last changes fastest.
Arguments:
- table: bfloat16 [16384, 512], P('wide'), may hold values from -6 to 6
- item_owner: int32 [65536, 1], P(('wide', 'narrow')), may hold values from 0 to 63; in each aligned block of 128 rows (0 to 127, 128 to 255, ...) at most 8 rows name the same one
- item_row: int32 [65536], P(('wide', 'narrow')), may hold values from 0 to 255
- lengths: int32 [512, 6], P(('wide', 'narrow')), may hold values from 1 to 64, 128 in all within a row
- cotangent: bfloat16 [65536, 512], P(('wide', 'narrow')), may hold values from -24 to 24
- w_uvqk: bfloat16 [512, 2048], replicated, may hold values from -0.25 to 0.25
- w_out: bfloat16 [512, 512], replicated, may hold values from -0.25 to 0.25
Outputs:
- grad_table: float32 [16384, 512], P('wide')
- grad_uvqk: float32 [512, 2048], P('narrow', 'wide')
- grad_out: float32 [512, 512], P('narrow', 'wide')
The draws below stay inside these ranges and needn't reach their ends.
Inputs may be any that keep to these rules, and one draw needn't show every extreme that they name: `item_owner`: among the actions of one block, at most 8 name the same owner, and some blocks reach 8. `lengths`: each row sums to 128 and its largest entry is 64.
All inputs are finite; a program needn't handle non-finite values.
Results may differ from the reference program's by a relative error of at most 0.024.
Values may be sent and summed in bfloat16 or wider, within the bound.
A program may use at most 64 MiB of HBM per device.

```python
import math
import jax
import jax.numpy as jnp
import numpy as np
from jax import lax

D = 512
HEADS = 8
TOK_DEV = 128
SEQ_DEV = 6
LMAX = 64
ROWS_DEV = 256
CAP = 8
TOKENS = 65536
TABLE_ROWS = 16384
N_WIDE = 64
N_NARROW = 8


def touch_ends(values, rng, low, top_value):
    longest = values.shape.index(max(values.shape))
    spots = []
    for shift in (0, 1):
        where = [jax.random.randint(jax.random.fold_in(rng, axis), (), 0, length) for axis, length in enumerate(values.shape)]
        where[longest] = (where[longest] + shift) % values.shape[longest]
        spots.append(tuple(where))
    return values.at[spots[0]].set(low).at[spots[1]].set(top_value)


def spiked(result, own_key, source, target, shards_of, factor):
    owner, partner = [(jnp.arange(result.shape[position]) // (result.shape[position] // shards_of)).reshape([-1 if axis == position else 1 for axis in range(result.ndim)]) for position in (source, target)]
    chosen = jax.random.permutation(own_key, shards_of)[partner]
    strong = (owner == chosen) | (owner == (partner + shards_of // 2) % shards_of)
    return jnp.where(strong, factor * result, result)


def steps_of(stream_key, extent, cuts, least, top_value):
    factor_of, own = 1.0, jax.random.fold_in(stream_key, 6)
    for dim, blocks in cuts:
        draws = jnp.exp(jax.random.uniform(jax.random.fold_in(own, dim), (blocks,), jnp.float32, least / len(cuts), top_value / len(cuts)))
        factor_of = factor_of * jnp.repeat(draws, extent[dim] // blocks).reshape([-1 if axis == dim else 1 for axis in range(len(extent))])
    return factor_of


def split_up(count, total, reach, skew):
    weights = [(1 << 20) // math.isqrt(rank ** skew) + 1 for rank in range(2, count + 1)]
    spare, counts = total - reach - (count - 1), [1] * (count - 1)
    while spare > 0:
        movable = [i for i in range(count - 1) if counts[i] < reach]
        pool, remaining = sum([weights[i] for i in movable]), spare
        for i in movable:
            addition = min(reach - counts[i], max(1, remaining * weights[i] // pool), spare)
            counts[i] = counts[i] + addition
            spare = spare - addition
    return np.array([reach] + counts)


def uneven(stream_key, count, total, bound, skew):
    if count == 2:
        one = jax.random.randint(stream_key, (), max(1, total - bound), min(bound, total - 1) + 1)
        return jnp.stack([one, total - one])
    sizes = jnp.asarray(split_up(count, total, bound, skew), jnp.int32)
    twos = (count - 1) // 2
    giver, receiver = sizes[1:1 + 2 * twos:2], sizes[2:2 + 2 * twos:2]
    room = jnp.minimum(giver - 1, bound - receiver)
    passed = jax.random.randint(jax.random.fold_in(stream_key, 1), (twos,), 0, 1 << 20) % (room + 1)
    sizes = sizes.at[1:1 + 2 * twos:2].set(giver - passed).at[2:2 + 2 * twos:2].set(receiver + passed)
    return sizes[jax.random.permutation(jax.random.fold_in(stream_key, 2), count)]


def assign_block(key, own, number, rows, count, top, most, slope):
    order = jax.random.permutation(key, count)
    crowded, ordinary = portions_of(count, rows * top, most, slope, True), portions_of(count, rows * top, most, slope, False)
    places = jnp.arange(count)

    def named(sizes, offset_by):
        used = int((sizes > 0).sum())
        fixed = max(1, used // 4)
        shifted = fixed + (places - fixed + offset_by * (used - fixed)) % max(1, count - fixed)
        return jnp.zeros((count,), jnp.int32).at[order[jnp.where(places < fixed, places, shifted)]].set(jnp.asarray(sizes, jnp.int32))

    sizes = jnp.where(number % 4 == 0, named(crowded, number // 4), named(ordinary, number - number // 4 - 1))
    mixed = jax.random.permutation(jax.random.fold_in(own, 3), count)
    donor, sink = mixed[0:count // 2 * 2:2], mixed[1:count // 2 * 2:2]
    slack = jnp.minimum(sizes[donor] - 1, most - sizes[sink]) // 2
    slack = jnp.where((donor == order[0]) | (sink == order[0]) | (sizes[sink] == 0), 0, jnp.maximum(slack, 0))
    shifted = jax.random.randint(jax.random.fold_in(own, 4), (count // 2,), 0, 1 << 20) % (slack + 1)
    sizes = sizes.at[donor].add(-shifted).at[sink].add(shifted)
    members = jnp.searchsorted(jnp.cumsum(sizes), jnp.arange(rows * top), side="right").astype(jnp.int32)
    table = members.reshape(top, rows).T
    table = table[jax.random.permutation(jax.random.fold_in(own, 1), rows)]
    offset_by = jax.random.randint(jax.random.fold_in(own, 2), (rows, 1), 0, top)
    return jnp.take_along_axis(table, (jnp.arange(top)[None, :] + offset_by) % top, axis=1)


def portions_of(number_of, total, bound, slope, full):
    loads = [(1 << 20) // math.isqrt(grade ** slope) + 1 for grade in range(1, number_of + 1)]
    largest = bound if full else min(bound, max(-(-total // number_of), total * loads[0] // sum(loads)))
    least = 1 if total - largest >= number_of - 1 else 0
    counts, spare = [largest] + [least] * (number_of - 1), total - largest - least * (number_of - 1)
    while spare > 0:
        candidates = [i for i in range(1, number_of) if counts[i] < largest] or [i for i in range(1, number_of) if counts[i] < bound]
        pool, budget = sum([loads[i] for i in candidates]), spare
        for i in candidates:
            addition = min(bound - counts[i], max(1, budget * loads[i] // pool), spare)
            counts[i] = counts[i] + addition
            spare = spare - addition
    return np.array(counts)


def centred(own_key, extent, deviation, limit, pieces=(), held_as=jnp.bfloat16):
    array = deviation * jax.random.normal(own_key, extent, jnp.float32)
    if pieces:
        array = array * steps_of(own_key, extent, pieces, -0.22, 0.18)
    return jnp.clip(array, -limit, limit).astype(held_as)


def bell_draw_with(rng, shape, width, most, pieces, heavy, held_as=jnp.bfloat16):
    values = width * jax.random.normal(rng, shape, jnp.float32)
    if pieces:
        values = values * steps_of(rng, shape, pieces, -0.22, 0.18)
    return jnp.clip(spiked(values, jax.random.fold_in(rng, 3), *heavy), -most, most).astype(held_as)


def setup_inputs(seed: int = 0) -> dict:
    seeds = jax.random.split(jax.random.key(seed), 8)
    table = centred(seeds[0], (TABLE_ROWS, D), 1.0, 6.0, ((0, 64),))
    item_owner_keys = jax.random.split(jax.random.fold_in(seeds[1], 1), TOKENS // TOK_DEV)
    item_owner_turns = jax.random.permutation(jax.random.fold_in(seeds[1], 3), TOKENS // TOK_DEV)
    item_owner = jax.vmap(lambda own, number: assign_block(jax.random.fold_in(seeds[1], 2), own, number, TOK_DEV, N_WIDE, 1, CAP, 2))(item_owner_keys, item_owner_turns).reshape((TOKENS, 1))
    item_row = touch_ends(jax.random.randint(seeds[2], (TOKENS,), 0, ROWS_DEV), jax.random.fold_in(seeds[2], 1), 0, ROWS_DEV - 1).astype(jnp.int32)
    lengths = jax.vmap(lambda own: uneven(own, SEQ_DEV, TOK_DEV, LMAX, 2))(jax.random.split(seeds[3], (N_WIDE * N_NARROW))).reshape((N_WIDE * N_NARROW, SEQ_DEV)).astype(jnp.int32)
    cotangent = bell_draw_with(seeds[4], (TOKENS, D), 1.0, 24.0, ((0, 512),), (0, 1, 512, 6.0))
    w_uvqk = centred(seeds[5], (D, 4 * D), D ** -0.5, 0.25)
    w_out = centred(seeds[6], (D, D), D ** -0.5, 0.25)
    return {"table": table, "item_owner": item_owner, "item_row": item_row, "lengths": lengths, "cotangent": cotangent, "w_uvqk": w_uvqk, "w_out": w_out}


eps = 1e-05

def norm_rows(values):
    center = values - lax.optimization_barrier(jnp.mean(values, axis=-1, keepdims=True))
    spread = lax.optimization_barrier(jnp.mean(center * center, axis=-1, keepdims=True))
    return center * lax.rsqrt(spread + eps)

def pair_weights(seq_lengths, row_count):
    seq_ends = jnp.cumsum(seq_lengths).astype(jnp.int32)
    positions = jnp.arange(row_count, dtype=jnp.int32)
    segment = lax.optimization_barrier(jnp.sum((positions[:, None] >= seq_ends[None, :]).astype(jnp.int32), axis=1))
    owned = segment[:, None] == jnp.arange(seq_lengths.shape[0], dtype=jnp.int32)[None, :]
    own_length = lax.optimization_barrier(jnp.sum(jnp.where(owned, seq_lengths[None, :], 0), axis=1)).astype(jnp.float32)
    allowed = (segment[:, None] == segment[None, :]) & (positions[None, :] <= positions[:, None])
    return jnp.where(allowed, 1.0 / own_length[:, None], 0.0).astype(jnp.float32)

def local_forward(embedded, w_uvqk, w_out, pair_weight):
    row_count, model_width = embedded.shape
    head_size = model_width // HEADS
    normed = norm_rows(embedded).astype(jnp.bfloat16)
    activated = jax.nn.silu(jnp.dot(normed, w_uvqk, preferred_element_type=jnp.float32)).astype(jnp.bfloat16)
    gate_part, value_part, query_part, key_part = jnp.split(activated, 4, axis=1)
    query_heads = query_part.reshape(row_count, HEADS, head_size).astype(jnp.float32)
    key_heads = key_part.reshape(row_count, HEADS, head_size).astype(jnp.float32)
    value_heads = value_part.reshape(row_count, HEADS, head_size).astype(jnp.float32)
    scores = jnp.einsum('qhe,khe->hqk', query_heads, key_heads)
    attention = (jax.nn.silu(scores * head_size ** (-0.5)) * pair_weight[None]).astype(jnp.bfloat16)
    mixture = jnp.einsum('hqk,khe->qhe', attention.astype(jnp.float32), value_heads).reshape(row_count, model_width)
    gated_rows = (norm_rows(mixture) * gate_part.astype(jnp.float32)).astype(jnp.bfloat16)
    return embedded + jnp.dot(gated_rows, w_out, preferred_element_type=jnp.float32)

def reference(table, item_owner, item_row, lengths, cotangent, w_uvqk, w_out):
    device_count = N_WIDE * N_NARROW
    owners = item_owner[:, 0].reshape(device_count, TOK_DEV)
    row_ids = item_row.reshape(device_count, TOK_DEV)
    cot_blocks = cotangent.reshape(device_count, TOK_DEV, D)

    def device_step(totals, device_block):
        owner_block, row_block, seq_lengths, cot_block = device_block
        table_ids = (owner_block * ROWS_DEV + row_block).astype(jnp.int32)
        embedded = table[table_ids].astype(jnp.float32)
        pair_weight = pair_weights(seq_lengths, TOK_DEV)

        def forward_rows(embed_rows, first_weight, second_weight):
            return local_forward(embed_rows, first_weight, second_weight, pair_weight)
        layer_out, pullback = jax.vjp(forward_rows, embedded, w_uvqk, w_out)
        grad_embed, grad_first, grad_second = pullback(cot_block.astype(jnp.float32))
        table_sum, first_sum, second_sum = totals
        return ((table_sum.at[table_ids].add(grad_embed.astype(jnp.float32)), first_sum + grad_first.astype(jnp.float32), second_sum + grad_second.astype(jnp.float32)), None)
    starting = (jnp.zeros((TABLE_ROWS, D), jnp.float32), jnp.zeros((D, 4 * D), jnp.float32), jnp.zeros((D, D), jnp.float32))
    totals, unused = lax.scan(device_step, starting, (owners, row_ids, lengths, cot_blocks))
    return (totals[0], totals[1], totals[2])
```

```python
import functools

import jax
import jax.numpy as jnp
from jax import lax
from jax.experimental import pallas as pl
from jax.experimental.pallas import tpu as pltpu
from jax.sharding import PartitionSpec as P

HEADS = 8
EPS = 1e-05
MESH = pl.DeviceIdType.MESH
F32, BF16, I32 = jnp.float32, jnp.bfloat16, jnp.int32
VMEM_LIMIT = 48 * 1024 * 1024


def div(value, by):
    return lax.div(value, jnp.int32(by))


def rem(value, by):
    return lax.rem(value, jnp.int32(by))


def coordinates():
    wide, narrow = lax.axis_index("wide"), lax.axis_index("narrow")
    return div(wide, 16), rem(wide, 16), div(narrow, 2), rem(narrow, 2)


def shard_z(y, c, b):
    return 2 * (rem(y + 2 * b, 4) + 4 * c) + 1 - b


def holder_of(z):
    b = 1 - rem(z, 2)
    half = div(z, 2)
    y = rem(rem(half, 4) + 4 - 2 * b, 4)
    return 2 * y + div(half, 4), b


def member(rank, a):
    narrow, b = holder_of(rem(rank, 16))
    return div(rank, 16) * 16 + 2 * a + b, narrow


def signal(sem, device):
    pl.semaphore_signal(sem, inc=1, device_id=device, device_id_type=MESH)


def send(src, dst, send_sem, recv_sem, device):
    pltpu.make_async_remote_copy(
        src_ref=src, dst_ref=dst, send_sem=send_sem, recv_sem=recv_sem, device_id=device, device_id_type=MESH
    ).start()


def waiter(ref, send_sem, recv_sem, device):
    return pltpu.make_async_remote_copy(
        src_ref=ref, dst_ref=ref, send_sem=send_sem, recv_sem=recv_sem, device_id=device, device_id_type=MESH
    )


def iota(shape, dim):
    return lax.broadcasted_iota(I32, shape, dim)


def onehot(hits):
    return jnp.where(hits, 1.0, 0.0).astype(BF16)


def dot(left, right, contract=((1,), (0,))):
    return lax.dot_general(left, right, (contract, ((), ())), preferred_element_type=F32)


def ranks(owner_c, owner_r):
    sub, lane = iota((128, 128), 0), iota((128, 128), 1)
    same = owner_c == owner_r
    across = jnp.sum(jnp.where(same & (sub < lane), 1.0, 0.0), axis=0, keepdims=True)
    down = jnp.sum(jnp.where(same & (lane < sub), 1.0, 0.0), axis=1, keepdims=True)
    return down.astype(I32), across.astype(I32)


def halves_to_blocks(first, second):
    return jnp.concatenate([first.reshape(64, 8, 256), second.reshape(64, 8, 256)], axis=1).astype(BF16)


def fetch_kernel(
    owner_c, owner_r, row_c, table, replies, asked,
    shard, ask_out, reply_out, shard_send, shard_recv, ask_send, ask_recv, reply_send, reply_recv,
):
    x, z, y, c = coordinates()
    a, b = div(z, 2), rem(z, 2)
    narrow = 2 * y + c
    my_z = shard_z(y, c, b)
    me = x * 16 + my_z
    to_narrow, to_b = holder_of(z)
    is_source = to_narrow == narrow
    barrier = pltpu.get_barrier_semaphore()

    def greet(step, carry):
        signal(barrier, member(rem(me + step, 64), a))
        return carry

    lax.fori_loop(1, 64, greet, 0)
    signal(barrier, (x * 16 + my_z, narrow))

    _, rank_r = ranks(owner_c[...], owner_r[...])
    slots = onehot(iota((512, 128), 0) == owner_r[...] * 8 + rank_r)
    named = jnp.broadcast_to((row_c[...] + 1).astype(F32), (128, 128)).astype(BF16)
    ask_out[...] = dot(slots, named).reshape(64, 8, 128)

    pl.semaphore_wait(barrier, 63 + 8 * is_source.astype(I32))

    @pl.when(is_source)
    def _():
        def give(step, carry):
            for half in range(2):
                send(
                    table.at[:, pl.ds(256 * half, 256)], shard.at[half],
                    shard_send.at[half], shard_recv.at[half], (x * 16 + 2 * step + to_b, narrow),
                )
            return carry

        lax.fori_loop(0, 8, give, 0)

    def ask(step, carry):
        rank = rem(me + step, 64)
        send(ask_out.at[rank], asked.at[me], ask_send, ask_recv, member(rank, a))
        return carry

    lax.fori_loop(1, 64, ask, 0)
    asked[pl.ds(me, 1)] = ask_out[pl.ds(me, 1)]
    here = (lax.axis_index("wide"), narrow)
    most = asked.at[pl.ds(0, 63)]
    waiter(most, ask_send, ask_recv, here).wait_recv()
    wanted = asked[...].reshape(512, 128).astype(I32)
    wanted = jnp.concatenate([wanted, wanted], axis=1)
    chosen = onehot(wanted == iota((512, 256), 1) + 1)
    for half in range(2):
        waiter(shard.at[half], shard_send.at[half], shard_recv.at[half], here).wait_recv()
    reply_out[...] = halves_to_blocks(dot(chosen, shard[0]), dot(chosen, shard[1]))

    def answer(step, carry):
        rank = rem(me + step, 64)
        send(reply_out.at[rank], replies.at[me], reply_send, reply_recv, member(rank, a))
        return carry

    lax.fori_loop(1, 64, answer, 0)
    replies[pl.ds(me, 1)] = reply_out[pl.ds(me, 1)]
    waiter(most, ask_send, ask_recv, here).wait_send()

    @pl.when(is_source)
    def _():
        def given(step, carry):
            for half in range(2):
                waiter(shard.at[half], shard_send.at[half], shard_recv.at[half], here).wait_send()
            return carry

        lax.fori_loop(0, 8, given, 0)

    waiter(replies.at[pl.ds(0, 63)], reply_send, reply_recv, here).wait()


def mean_rows(values):
    return jnp.mean(values, axis=-1, keepdims=True)


def norm_back(grad, normed, scale):
    return scale * (grad - mean_rows(grad) - normed * mean_rows(grad * normed))


def layer_kernel(lengths, owner_c, owner_r, replies, cotangent, w_uvqk, w_out, outgoing, grad_u, grad_o, pre, act, grad_act):
    rank_c, rank_r = ranks(owner_c[...], owner_r[...])
    slot_c = owner_c[...] * 16 + rank_c
    spots = iota((128, 1024), 1)
    arrived = replies[...]
    embedded = jnp.concatenate(
        [dot(onehot(spots == slot_c), arrived), dot(onehot(spots == slot_c + 8), arrived)], axis=1
    )
    center = embedded - mean_rows(embedded)
    embed_scale = lax.rsqrt(mean_rows(center * center) + EPS)
    embed_norm = center * embed_scale
    normed = embed_norm.astype(BF16)

    for part in range(4):
        cols = pl.ds(512 * part, 512)
        value = dot(normed, w_uvqk[:, cols])
        pre[:, cols] = value
        act[:, cols] = (value * jax.nn.sigmoid(value)).astype(BF16)

    sub, lane = iota((128, 128), 0), iota((128, 128), 1)
    seg_t, seg_s, total = jnp.zeros((128, 128), I32), jnp.zeros((128, 128), I32), jnp.int32(0)
    for i in range(6):
        total = total + lengths[0, i]
        seg_t = seg_t + jnp.where(sub >= total, 1, 0)
        seg_s = seg_s + jnp.where(lane >= total, 1, 0)
    own_length = jnp.ones((128, 128), F32)
    for i in range(6):
        own_length = jnp.where(seg_t == i, lengths[0, i].astype(F32), own_length)
    weight = jnp.where((seg_t == seg_s) & (lane <= sub), 1.0 / own_length, 0.0)

    first_half = lane < 64
    keep = (first_half, jnp.logical_not(first_half))
    zero = jnp.zeros((128, 128), BF16)
    mixed = []
    for pair in range(4):
        q = act[:, 1024 + 128 * pair : 1152 + 128 * pair]
        k = act[:, 1536 + 128 * pair : 1664 + 128 * pair]
        v = act[:, 512 + 128 * pair : 640 + 128 * pair]
        both = jnp.zeros((128, 128), F32)
        for head in range(2):
            score = dot(jnp.where(keep[head], q, zero), k, ((1,), (1,))) * 0.125
            attention = (score * jax.nn.sigmoid(score) * weight).astype(BF16)
            both = both + dot(attention, jnp.where(keep[head], v, zero))
        mixed.append(both)
    mixture = jnp.concatenate(mixed, axis=1)
    center = mixture - mean_rows(mixture)
    mix_scale = lax.rsqrt(mean_rows(center * center) + EPS)
    mix_norm = center * mix_scale
    gate = act[:, 0:512].astype(F32)
    gated = (mix_norm * gate).astype(BF16)

    cot = cotangent[...]
    grad_o[...] = dot(cot, gated, ((0,), (0,))).astype(BF16)
    grad_gated = dot(cot, w_out[...], ((1,), (1,)))
    grad_act[:, 0:512] = grad_gated * mix_norm
    grad_mix = norm_back(grad_gated * gate, mix_norm, mix_scale).astype(BF16)
    for pair in range(4):
        q = act[:, 1024 + 128 * pair : 1152 + 128 * pair]
        k = act[:, 1536 + 128 * pair : 1664 + 128 * pair]
        v = act[:, 512 + 128 * pair : 640 + 128 * pair]
        g = grad_mix[:, 128 * pair : 128 * pair + 128]
        grad_q, grad_k, grad_v = [jnp.zeros((128, 128), F32)] * 3
        for head in range(2):
            q_one, k_one, v_one, g_one = [jnp.where(keep[head], part, zero) for part in (q, k, v, g)]
            score = dot(q_one, k, ((1,), (1,))) * 0.125
            gain = jax.nn.sigmoid(score)
            attention = (score * gain * weight).astype(BF16)
            grad_att = dot(g_one, v, ((1,), (1,)))
            grad_score = (grad_att * weight * (gain * (1.0 + score * (1.0 - gain))) * 0.125).astype(BF16)
            grad_v = grad_v + dot(attention, g_one, ((0,), (0,)))
            grad_q = grad_q + dot(grad_score, k_one)
            grad_k = grad_k + dot(grad_score, q_one, ((0,), (0,)))
        grad_act[:, 512 + 128 * pair : 640 + 128 * pair] = grad_v
        grad_act[:, 1024 + 128 * pair : 1152 + 128 * pair] = grad_q
        grad_act[:, 1536 + 128 * pair : 1664 + 128 * pair] = grad_k

    grad_normed = jnp.zeros((128, 512), F32)
    for part in range(4):
        cols = pl.ds(512 * part, 512)
        value = pre[:, cols]
        gain = jax.nn.sigmoid(value)
        grad_pre = (grad_act[:, cols] * (gain * (1.0 + value * (1.0 - gain)))).astype(BF16)
        grad_normed = grad_normed + dot(grad_pre, w_uvqk[:, cols], ((1,), (1,)))
        grad_u[cols, :] = dot(grad_pre, normed, ((0,), (0,))).astype(BF16)
    grad_embed = cot.astype(F32) + norm_back(grad_normed, embed_norm, embed_scale)
    grad_embed = grad_embed.astype(BF16)
    slots = onehot(iota((512, 128), 0) == owner_r[...] * 8 + rank_r)
    outgoing[...] = halves_to_blocks(dot(slots, grad_embed[:, 0:256]), dot(slots, grad_embed[:, 256:512]))


def reduce_kernel(
    outgoing, asked, grad_u, grad_o, out_table, out_u, out_o,
    rows_in, pair_in, plane_out, plane_in, line_out, line_in, piece_out, piece_in, share, turned,
    rows_send, rows_recv, pair_send, pair_recv, plane_send, plane_recv, line_send, line_recv,
    piece_send, piece_recv, share_send, share_recv,
):
    x, z, y, c = coordinates()
    wide = x * 16 + z
    a, b = div(z, 2), rem(z, 2)
    narrow = 2 * y + c
    my_z = shard_z(y, c, b)
    me = x * 16 + my_z
    from_narrow, from_b = holder_of(z)
    upper = div(z, 8)
    here = (wide, narrow)
    in_half = (upper == c).astype(I32)
    barrier = pltpu.get_barrier_semaphore()

    def greet(step, carry):
        signal(barrier, member(rem(me + step, 64), a))
        return carry

    lax.fori_loop(1, 64, greet, 0)

    def greet_line(step, carry):
        signal(barrier, (x * 16 + 2 * step + from_b, from_narrow))
        return carry

    lax.fori_loop(0, 8, greet_line, 0)

    def greet_column(step, carry):
        @pl.when(jnp.logical_or(step != z, upper != c))
        def _():
            signal(barrier, (x * 16 + step, 2 * y + upper))

        return carry

    lax.fori_loop(0, 16, greet_column, 0)
    pl.semaphore_wait(barrier, 63 + 8 + 16 - in_half)

    partner = (wide, 2 * y + 1 - c)
    for part in range(4):
        send(
            grad_u.at[pl.ds(512 * part + 256 * (1 - c), 256)], pair_in.at[part, pl.ds(0, 256)],
            pair_send, pair_recv, partner,
        )
        send(
            grad_o.at[pl.ds(128 * part + 64 * (1 - c), 64)], pair_in.at[part, pl.ds(256, 64)],
            pair_send, pair_recv, partner,
        )

    def give_rows(step, carry):
        rank = rem(me + step, 64)
        send(outgoing.at[rank], rows_in.at[me], rows_send, rows_recv, member(rank, a))
        return carry

    lax.fori_loop(1, 64, give_rows, 0)
    rows_in[pl.ds(me, 1)] = outgoing[pl.ds(me, 1)]

    waiter(pair_in, pair_send, pair_recv, here).wait()
    for part in range(4):
        mine = grad_u[pl.ds(512 * part + 256 * c, 256), :].astype(F32)
        plane_out[part, 0:256] = (mine + pair_in[part, 0:256].astype(F32)).astype(BF16)
        mine = grad_o[pl.ds(128 * part + 64 * c, 64), :].astype(F32)
        plane_out[part, 256:320] = (mine + pair_in[part, 256:320].astype(F32)).astype(BF16)

    spot = 4 * x + y

    def give_plane(step, carry):
        to = rem(spot + step, 16)
        to_x, to_y = div(to, 4), rem(to, 4)
        send(
            plane_out.at[to_x, :, pl.ds(pl.multiple_of(128 * to_y, 128), 128)], plane_in.at[spot],
            plane_send, plane_recv, (to_x * 16 + z, 2 * to_y + c),
        )
        return carry

    lax.fori_loop(1, 16, give_plane, 0)
    plane_in[pl.ds(spot, 1)] = plane_out[pl.ds(x, 1), :, pl.ds(pl.multiple_of(128 * y, 128), 128)]

    waiter(rows_in.at[pl.ds(0, 63)], rows_send, rows_recv, here).wait()
    wanted = asked[...].reshape(512, 128).astype(I32)
    wanted = jnp.concatenate([wanted, wanted], axis=1)
    chosen = onehot(wanted == iota((512, 256), 1) + 1)
    arrived = rows_in[...].astype(F32)
    for half in range(2):
        rows = arrived[:, 8 * half : 8 * half + 8].reshape(512, 256).astype(BF16)
        sums = dot(chosen, rows, ((0,), (0,))).astype(BF16)
        for piece in range(8):
            piece_out[piece, 32 * half : 32 * half + 32] = sums[32 * piece : 32 * piece + 32]

    def give_piece(step, carry):
        to = rem(narrow + step, 8)
        send(piece_out.at[to], piece_in.at[a], piece_send, piece_recv, (x * 16 + my_z, to))
        return carry

    lax.fori_loop(0, 8, give_piece, 0)

    waiter(plane_in.at[pl.ds(0, 15)], plane_send, plane_recv, here).wait()
    total = plane_in[0].astype(F32)
    for step in range(1, 16):
        total = total + plane_in[step].astype(F32)
    for step in range(8):
        line_out[step] = jnp.concatenate(
            [total[32 * step : 32 * step + 32], total[256 + 8 * step : 264 + 8 * step], jnp.zeros((8, 128), F32)], axis=0
        ).astype(BF16)

    def give_line(step, carry):
        to_z = 8 * c + step
        for core in range(2):
            own = jnp.logical_and(to_z == z, c == core)

            @pl.when(jnp.logical_not(own))
            def _():
                send(line_out.at[step], line_in.at[z], line_send, line_recv, (x * 16 + to_z, 2 * y + core))

            @pl.when(own)
            def _():
                line_in[pl.ds(z, 1)] = line_out[pl.ds(step, 1)]

        return carry

    lax.fori_loop(0, 8, give_line, 0)

    waiter(piece_in, piece_send, piece_recv, here).wait()
    total = piece_in[0].astype(F32)
    for step in range(1, 8):
        total = total + piece_in[step].astype(F32)
    share[pl.ds(narrow, 1)] = total.astype(BF16).reshape(1, 64, 256)

    def give_share(step, carry):
        send(share.at[narrow], share.at[narrow], share_send, share_recv, (wide, rem(narrow + step, 8)))
        return carry

    lax.fori_loop(1, 8, give_share, 0)

    @pl.when(in_half == 1)
    def _():
        waiter(line_in.at[pl.ds(0, 15)], line_send, line_recv, here).wait()

    @pl.when(in_half == 0)
    def _():
        waiter(line_in, line_send, line_recv, here).wait()

    total = line_in[0].astype(F32)
    for step in range(1, 16):
        total = total + line_in[step].astype(F32)
    turned[...] = jnp.concatenate([total, jnp.zeros((80, 128), F32)], axis=0).T
    mine = turned[pl.ds(pl.multiple_of(64 * c, 64), 64), :]
    out_u[...] = mine[:, 0:32]
    out_o[...] = mine[:, 32:40]

    waiter(share.at[pl.ds(0, 7)], share_send, share_recv, here).wait()
    for piece in range(8):
        out_table[32 * piece : 32 * piece + 32, 0:256] = share[piece, 0:32].astype(F32)
        out_table[32 * piece : 32 * piece + 32, 256:512] = share[piece, 32:64].astype(F32)


def on_device(table, item_owner, item_row, lengths, cotangent, w_uvqk, w_out):
    owner_c, owner_r, row_c = item_owner, item_owner.reshape(1, 128), item_row.reshape(128, 1)
    vmem = pl.BlockSpec(memory_space=pltpu.VMEM)
    smem = pl.BlockSpec(memory_space=pltpu.SMEM)
    dma = pltpu.SemaphoreType.DMA
    shape = jax.ShapeDtypeStruct

    replies, asked = pl.pallas_call(
        fetch_kernel,
        out_shape=(shape((64, 16, 256), BF16), shape((64, 8, 128), F32)),
        in_specs=[vmem] * 4,
        out_specs=(vmem, vmem),
        scratch_shapes=[
            pltpu.VMEM((2, 256, 256), BF16),
            pltpu.VMEM((64, 8, 128), F32),
            pltpu.VMEM((64, 16, 256), BF16),
            dma((2,)), dma((2,)), dma, dma, dma, dma,
        ],
        compiler_params=pltpu.CompilerParams(collective_id=0, has_side_effects=True, vmem_limit_bytes=VMEM_LIMIT),
        name="fetch_rows",
    )(owner_c, owner_r, row_c, table)

    outgoing, grad_u, grad_o = pl.pallas_call(
        layer_kernel,
        out_shape=(shape((64, 16, 256), BF16), shape((2048, 512), BF16), shape((512, 512), BF16)),
        in_specs=[smem] + [vmem] * 6,
        out_specs=(vmem,) * 3,
        scratch_shapes=[pltpu.VMEM((128, 2048), F32), pltpu.VMEM((128, 2048), BF16), pltpu.VMEM((128, 2048), F32)],
        compiler_params=pltpu.CompilerParams(vmem_limit_bytes=VMEM_LIMIT),
        name="layer",
    )(lengths, owner_c, owner_r, replies.reshape(1024, 256), cotangent, w_uvqk, w_out)

    return pl.pallas_call(
        reduce_kernel,
        out_shape=(shape((256, 512), F32), shape((64, 32), F32), shape((64, 8), F32)),
        in_specs=[vmem] * 4,
        out_specs=(vmem,) * 3,
        scratch_shapes=[
            pltpu.VMEM((64, 16, 256), BF16),
            pltpu.VMEM((4, 320, 512), BF16),
            pltpu.VMEM((4, 320, 512), BF16),
            pltpu.VMEM((16, 320, 128), BF16),
            pltpu.VMEM((8, 48, 128), BF16),
            pltpu.VMEM((16, 48, 128), BF16),
            pltpu.VMEM((8, 64, 256), BF16),
            pltpu.VMEM((8, 64, 256), BF16),
            pltpu.VMEM((8, 64, 256), BF16),
            pltpu.VMEM((128, 128), F32),
        ] + [dma] * 12,
        compiler_params=pltpu.CompilerParams(collective_id=1, has_side_effects=True, vmem_limit_bytes=VMEM_LIMIT),
        name="reduce_grads",
    )(outgoing, asked, grad_u, grad_o)


def solution(mesh):
    in_specs = (
        P("wide", None),
        P(("wide", "narrow"), None),
        P(("wide", "narrow")),
        P(("wide", "narrow"), None),
        P(("wide", "narrow"), None),
        P(),
        P(),
    )
    out_specs = (P("wide", None), P("narrow", "wide"), P("narrow", "wide"))
    return jax.shard_map(on_device, mesh=mesh, in_specs=in_specs, out_specs=out_specs, check_vma=False)
```

```python
import jax
import jax.numpy as jnp
from jax import lax
from jax.experimental import pallas as pl
from jax.experimental.pallas import tpu as pltpu
from jax.sharding import PartitionSpec as P

HEADS = 8
EPS = 1e-05
MESH = pl.DeviceIdType.MESH
F32, BF16, I32 = jnp.float32, jnp.bfloat16, jnp.int32
VMEM_LIMIT = 63 * 1024 * 1024


def div(value, by):
    return lax.div(value, jnp.int32(by))


def rem(value, by):
    return lax.rem(value, jnp.int32(by))


def coordinates():
    wide, narrow = lax.axis_index("wide"), lax.axis_index("narrow")
    return div(wide, 16), rem(wide, 16), div(narrow, 2), rem(narrow, 2)


def shard_z(y, c, b):
    return 2 * (rem(y + 2 * b, 4) + 4 * c) + 1 - b


def holder_of(z):
    b = 1 - rem(z, 2)
    half = div(z, 2)
    y = rem(rem(half, 4) + 4 - 2 * b, 4)
    return 2 * y + div(half, 4), b


def member(rank, a):
    narrow, b = holder_of(rem(rank, 16))
    return div(rank, 16) * 16 + 2 * a + b, narrow


def signal(sem, device):
    pl.semaphore_signal(sem, inc=1, device_id=device, device_id_type=MESH)


def send(src, dst, send_sem, recv_sem, device):
    pltpu.make_async_remote_copy(
        src_ref=src, dst_ref=dst, send_sem=send_sem, recv_sem=recv_sem, device_id=device, device_id_type=MESH
    ).start()


def waiter(ref, send_sem, recv_sem, device):
    return pltpu.make_async_remote_copy(
        src_ref=ref, dst_ref=ref, send_sem=send_sem, recv_sem=recv_sem, device_id=device, device_id_type=MESH
    )


def iota(shape, dim):
    return lax.broadcasted_iota(I32, shape, dim)


def onehot(hits):
    return jnp.where(hits, 1.0, 0.0).astype(BF16)


def dot(left, right, contract=((1,), (0,))):
    return lax.dot_general(left, right, (contract, ((), ())), preferred_element_type=F32)


def ranks(owner_t, owner_s):
    sub, lane = iota((128, 128), 0), iota((128, 128), 1)
    same = owner_t == owner_s
    across = jnp.sum(jnp.where(same & (sub < lane), 1.0, 0.0), axis=0, keepdims=True)
    down = jnp.sum(jnp.where(same & (lane < sub), 1.0, 0.0), axis=1, keepdims=True)
    return down, across


def to_blocks(first, second):
    return jnp.concatenate([first.reshape(64, 8, 128), second.reshape(64, 8, 128)], axis=1).astype(BF16)


def from_blocks(blocks):
    values = blocks.astype(F32)
    return jnp.concatenate([values[:, 0:8].reshape(512, 128), values[:, 8:16].reshape(512, 128)], axis=1).astype(BF16)


def mean_rows(values):
    return jnp.mean(values, axis=-1, keepdims=True)


def norm_back(grad, normed, scale):
    return scale * (grad - mean_rows(grad) - normed * mean_rows(grad * normed))


def weights_of_pairs(lengths):
    sub, lane = iota((128, 128), 0), iota((128, 128), 1)
    seg_t, seg_s = jnp.zeros((128, 128), I32), jnp.zeros((128, 128), I32)
    total = jnp.zeros((1, 1), I32)
    for i in range(6):
        total = total + lengths[0:1, i : i + 1]
        seg_t = seg_t + jnp.where(sub >= total, 1, 0)
        seg_s = seg_s + jnp.where(lane >= total, 1, 0)
    own_length = jnp.ones((128, 128), F32)
    for i in range(6):
        own_length = jnp.where(seg_t == i, lengths[0:1, i : i + 1].astype(F32), own_length)
    return jnp.where((seg_t == seg_s) & (lane <= sub), 1.0 / own_length, 0.0)


def layer_kernel(
    owner_hbm, row_hbm, lengths_hbm, table, cotangent_hbm, w_uvqk_hbm, w_out_hbm, out_table, out_u, out_o,
    owner, row, lengths, cotangent, w_uvqk, w_out, shard, ask_out, asked, chosen, reply_out, replies,
    pre, act, grad_act, grads, rows_out, rows_in, pair_in, plane_out, x_in, y_in, x_mid, y_mid, xy_in, yx_in,
    line_out, line_in, piece_out, piece_in, share, turned,
    load_sem, shard_send, shard_recv, relay_send, ask_send, ask_recv, reply_send, reply_recv,
    rows_send, rows_recv, pair_send, pair_recv, plane_send, plane_recv, line_send, line_recv,
    piece_send, piece_recv, share_send, share_recv,
):
    x, z, y, c = coordinates()
    wide = x * 16 + z
    a, b = div(z, 2), rem(z, 2)
    narrow = 2 * y + c
    here = (wide, narrow)
    my_z = shard_z(y, c, b)
    me = x * 16 + my_z
    to_narrow, to_b = holder_of(z)
    is_source = to_narrow == narrow
    away = rem(z - my_z + 16, 16)
    is_relay = jnp.logical_or(away == 3, away == 13)
    outward = jnp.where(away == 3, 1, -1)
    upper = div(z, 8)
    in_half = (upper == c).astype(I32)
    barrier = pltpu.get_barrier_semaphore()

    def on_line(at_z):
        return x * 16 + rem(at_z + 32, 16), narrow

    loads = []
    for i, (src, dst) in enumerate(
        [(owner_hbm, owner), (row_hbm, row), (lengths_hbm, lengths), (w_uvqk_hbm, w_uvqk), (cotangent_hbm, cotangent), (w_out_hbm, w_out)]
    ):
        loads.append(pltpu.make_async_copy(src, dst, load_sem.at[i]))
        loads[-1].start()

    parent = jnp.where(
        jnp.logical_or(away == 5, away == 7), my_z + 3, jnp.where(jnp.logical_or(away == 9, away == 11), my_z - 3, my_z)
    )
    signal(barrier, on_line(parent))

    def greet_line(step, carry):
        signal(barrier, (x * 16 + 2 * step + to_b, to_narrow))
        return carry

    lax.fori_loop(0, 8, greet_line, 0)

    def greet_column(step, carry):
        @pl.when(jnp.logical_or(step != z, upper != c))
        def _():
            signal(barrier, (x * 16 + step, 2 * y + upper))

        return carry

    lax.fori_loop(0, 16, greet_column, 0)

    def greet(step, carry):
        signal(barrier, member(rem(me + step, 64), a))
        return carry

    lax.fori_loop(1, 64, greet, 0)

    loads[0].wait()
    loads[1].wait()
    owner_s = jnp.broadcast_to(owner[...].astype(F32), (128, 128))
    owner_t = owner_s.T
    rank_t, rank_s = ranks(owner_t, owner_s)
    slot_s = (owner_s * 8.0 + rank_s)[0:1].astype(I32)
    slot_t = (owner_t * 16.0 + rank_t)[:, 0:1].astype(I32)
    slots = onehot(iota((512, 128), 0) == slot_s)
    named = (jnp.broadcast_to(row[...].astype(F32), (128, 128)).T + 1.0).astype(BF16)
    ask_out[...] = dot(slots, named).reshape(64, 8, 128)

    pl.semaphore_wait(barrier, 63 + 8 + 16 - in_half + 4 * is_source.astype(I32) + 2 * is_relay.astype(I32))

    for half in range(2):

        @pl.when(is_source)
        def _(half=half):
            for step in (3, -3, 1, -1):
                send(
                    table.at[:, pl.ds(256 * half, 256)], shard.at[half],
                    shard_send.at[half], shard_recv.at[half], on_line(z + step),
                )

    def ask(step, carry):
        rank = rem(me + step, 64)
        send(ask_out.at[rank], asked.at[me], ask_send, ask_recv, member(rank, a))
        return carry

    lax.fori_loop(1, 64, ask, 0)
    asked[pl.ds(me, 1)] = ask_out[pl.ds(me, 1)]
    most = pl.ds(0, 63)

    def relay(half):
        waiter(shard.at[half], shard_send.at[half], shard_recv.at[half], here).wait_recv()

        @pl.when(is_relay)
        def _():
            for step in (4, 2):
                send(
                    shard.at[half], shard.at[half],
                    relay_send.at[half], shard_recv.at[half], on_line(z + outward * step),
                )

    relay(0)
    waiter(asked.at[most], ask_send, ask_recv, here).wait_recv()
    wanted = asked[...].reshape(512, 128).astype(I32)
    wanted = jnp.concatenate([wanted, wanted], axis=1)
    chosen[...] = onehot(wanted == iota((512, 256), 1) + 1)
    for half in range(2):
        if half:
            relay(half)
        picked = dot(chosen[...], shard[half])
        reply_out[half] = to_blocks(picked[:, 0:128], picked[:, 128:256])

        def answer(step, carry, half=half):
            rank = rem(me + step, 64)
            send(
                reply_out.at[half, rank], replies.at[half, me],
                reply_send.at[half], reply_recv.at[half], member(rank, a),
            )
            return carry

        lax.fori_loop(1, 64, answer, 0)
        replies[half, pl.ds(me, 1)] = reply_out[half, pl.ds(me, 1)]

    loads[2].wait()
    weight = weights_of_pairs(lengths)
    spots = iota((128, 1024), 1)
    finds = (onehot(spots == slot_t), onehot(spots == slot_t + 8))
    parts = []
    for half in range(2):
        waiter(replies.at[half, most], reply_send.at[half], reply_recv.at[half], here).wait_recv()
        arrived = replies[half].reshape(1024, 128)
        parts += [dot(finds[0], arrived), dot(finds[1], arrived)]
    embedded = jnp.concatenate(parts, axis=1)
    center = embedded - mean_rows(embedded)
    embed_scale = lax.rsqrt(mean_rows(center * center) + EPS)
    embed_norm = center * embed_scale
    normed = embed_norm.astype(BF16)

    loads[3].wait()
    for part in range(4):
        cols = pl.ds(512 * part, 512)
        value = dot(normed, w_uvqk[:, cols])
        pre[:, cols] = value
        act[:, cols] = (value * jax.nn.sigmoid(value)).astype(BF16)

    first_half = iota((128, 128), 1) < 64
    keep = (first_half, jnp.logical_not(first_half))
    zero = jnp.zeros((128, 128), BF16)
    mixed = []
    for pair in range(4):
        q = act[:, 1024 + 128 * pair : 1152 + 128 * pair]
        k = act[:, 1536 + 128 * pair : 1664 + 128 * pair]
        v = act[:, 512 + 128 * pair : 640 + 128 * pair]
        both = jnp.zeros((128, 128), F32)
        for head in range(2):
            score = dot(jnp.where(keep[head], q, zero), k, ((1,), (1,))) * 0.125
            attention = (score * jax.nn.sigmoid(score) * weight).astype(BF16)
            both = both + dot(attention, jnp.where(keep[head], v, zero))
        mixed.append(both)
    mixture = jnp.concatenate(mixed, axis=1)
    center = mixture - mean_rows(mixture)
    mix_scale = lax.rsqrt(mean_rows(center * center) + EPS)
    mix_norm = center * mix_scale
    gate = act[:, 0:512].astype(F32)
    gated = (mix_norm * gate).astype(BF16)

    loads[4].wait()
    loads[5].wait()
    cot = cotangent[...]
    grad_o = dot(cot, gated, ((0,), (0,))).astype(BF16)
    for part in range(4):
        for side in range(2):
            grads[part, side, 256:320] = grad_o[128 * part + 64 * side : 128 * part + 64 * side + 64]

    partner = (wide, 2 * y + 1 - c)

    def back(part, grad_normed):
        cols = pl.ds(512 * part, 512)
        value = pre[:, cols]
        gain = jax.nn.sigmoid(value)
        grad_pre = (grad_act[:, cols] * (gain * (1.0 + value * (1.0 - gain)))).astype(BF16)
        grad_u = dot(grad_pre, normed, ((0,), (0,))).astype(BF16)
        for side in range(2):
            grads[part, side, 0:256] = grad_u[256 * side : 256 * side + 256]
        send(grads.at[part, 1 - c], pair_in.at[part], pair_send.at[part], pair_recv.at[part], partner)
        return grad_normed + dot(grad_pre, w_uvqk[:, cols], ((1,), (1,)))

    grad_gated = dot(cot, w_out[...], ((1,), (1,)))
    grad_act[:, 0:512] = grad_gated * mix_norm
    grad_normed = back(0, jnp.zeros((128, 512), F32))
    grad_mix = norm_back(grad_gated * gate, mix_norm, mix_scale).astype(BF16)
    for pair in range(4):
        q = act[:, 1024 + 128 * pair : 1152 + 128 * pair]
        k = act[:, 1536 + 128 * pair : 1664 + 128 * pair]
        v = act[:, 512 + 128 * pair : 640 + 128 * pair]
        g = grad_mix[:, 128 * pair : 128 * pair + 128]
        grad_q, grad_k, grad_v = [jnp.zeros((128, 128), F32)] * 3
        for head in range(2):
            q_one, k_one, v_one, g_one = [jnp.where(keep[head], part, zero) for part in (q, k, v, g)]
            score = dot(q_one, k, ((1,), (1,))) * 0.125
            gain = jax.nn.sigmoid(score)
            attention = (score * gain * weight).astype(BF16)
            grad_att = dot(g_one, v, ((1,), (1,)))
            grad_score = (grad_att * weight * (gain * (1.0 + score * (1.0 - gain))) * 0.125).astype(BF16)
            grad_v = grad_v + dot(attention, g_one, ((0,), (0,)))
            grad_q = grad_q + dot(grad_score, k_one)
            grad_k = grad_k + dot(grad_score, q_one, ((0,), (0,)))
        grad_act[:, 512 + 128 * pair : 640 + 128 * pair] = grad_v
        grad_act[:, 1024 + 128 * pair : 1152 + 128 * pair] = grad_q
        grad_act[:, 1536 + 128 * pair : 1664 + 128 * pair] = grad_k
    for part in range(1, 4):
        grad_normed = back(part, grad_normed)
    grad_embed = (cot.astype(F32) + norm_back(grad_normed, embed_norm, embed_scale)).astype(BF16)

    def give_rows(half):
        given = dot(slots, grad_embed[:, 256 * half : 256 * half + 256])
        rows_out[half] = to_blocks(given[:, 0:128], given[:, 128:256])

        def give(step, carry):
            rank = rem(me + step, 64)
            send(
                rows_out.at[half, rank], rows_in.at[half, me],
                rows_send.at[half], rows_recv.at[half], member(rank, a),
            )
            return carry

        lax.fori_loop(1, 64, give, 0)
        rows_in[half, pl.ds(me, 1)] = rows_out[half, pl.ds(me, 1)]

    give_rows(0)
    for part in range(4):
        waiter(pair_in.at[part], pair_send.at[part], pair_recv.at[part], here).wait()
        mine = grads[part, pl.ds(c, 1)].reshape(320, 512).astype(F32)
        plane_out[part] = (mine + pair_in[part].astype(F32)).astype(BF16)
    for step in range(1, 4):
        to_x, to_y = rem(x + step, 4), rem(y + step, 4)
        send(
            plane_out.at[to_x, pl.ds(0, 160)], x_in.at[x], plane_send.at[0], plane_recv.at[0],
            (to_x * 16 + z, narrow),
        )
        send(
            plane_out.at[:, pl.ds(160, 160), pl.ds(pl.multiple_of(128 * to_y, 128), 128)], y_in.at[y],
            plane_send.at[1], plane_recv.at[1], (wide, 2 * to_y + c),
        )
    my_lanes = pl.ds(pl.multiple_of(128 * y, 128), 128)
    x_in[pl.ds(x, 1)] = plane_out[pl.ds(x, 1), 0:160]
    y_in[pl.ds(y, 1)] = plane_out[:, 160:320, my_lanes].reshape(1, 4, 160, 128)
    give_rows(1)

    for half in range(2):
        waiter(rows_in.at[half, most], rows_send.at[half], rows_recv.at[half], here).wait()
        sums = dot(chosen[...], from_blocks(rows_in[half]), ((0,), (0,))).astype(BF16)
        for piece in range(8):
            piece_out[half, piece] = sums[32 * piece : 32 * piece + 32]

        def give_piece(step, carry, half=half):
            to = rem(narrow + step, 8)
            send(
                piece_out.at[half, to], piece_in.at[half, a],
                piece_send.at[half], piece_recv.at[half], (x * 16 + my_z, to),
            )
            return carry

        lax.fori_loop(0, 8, give_piece, 0)

    three = pl.ds(0, 3)

    def add_up(ref):
        total = ref[0].astype(F32)
        for step in range(1, ref.shape[0]):
            total = total + ref[step].astype(F32)
        return total

    waiter(x_in.at[three], plane_send.at[0], plane_recv.at[0], here).wait()
    x_mid[...] = add_up(x_in).astype(BF16)
    for step in range(1, 4):
        to_y = rem(y + step, 4)
        send(
            x_mid.at[:, pl.ds(pl.multiple_of(128 * to_y, 128), 128)], xy_in.at[y],
            plane_send.at[2], plane_recv.at[2], (wide, 2 * to_y + c),
        )
    xy_in[pl.ds(y, 1)] = x_mid[:, my_lanes].reshape(1, 160, 128)
    waiter(y_in.at[three], plane_send.at[1], plane_recv.at[1], here).wait()
    y_mid[...] = add_up(y_in).astype(BF16)
    for step in range(1, 4):
        to_x = rem(x + step, 4)
        send(y_mid.at[to_x], yx_in.at[x], plane_send.at[3], plane_recv.at[3], (to_x * 16 + z, narrow))
    yx_in[pl.ds(x, 1)] = y_mid[pl.ds(x, 1)]
    waiter(xy_in.at[three], plane_send.at[2], plane_recv.at[2], here).wait()
    waiter(yx_in.at[three], plane_send.at[3], plane_recv.at[3], here).wait()
    total = jnp.concatenate([add_up(xy_in), add_up(yx_in)], axis=0)
    for step in range(8):
        line_out[step] = jnp.concatenate(
            [total[32 * step : 32 * step + 32], total[256 + 8 * step : 264 + 8 * step], jnp.zeros((8, 128), F32)], axis=0
        ).astype(BF16)

    def give_line(step, carry):
        to_z = 8 * c + step
        for core in range(2):
            own = jnp.logical_and(to_z == z, c == core)

            @pl.when(jnp.logical_not(own))
            def _():
                send(line_out.at[step], line_in.at[z], line_send, line_recv, (x * 16 + to_z, 2 * y + core))

            @pl.when(own)
            def _():
                line_in[pl.ds(z, 1)] = line_out[pl.ds(step, 1)]

        return carry

    lax.fori_loop(0, 8, give_line, 0)

    for half in range(2):
        waiter(piece_in.at[half], piece_send.at[half], piece_recv.at[half], here).wait()
        share[half, pl.ds(narrow, 1)] = add_up(piece_in.at[half]).astype(BF16).reshape(1, 32, 256)

        def give_share(step, carry, half=half):
            send(
                share.at[half, narrow], share.at[half, narrow],
                share_send.at[half], share_recv.at[half], (wide, rem(narrow + step, 8)),
            )
            return carry

        lax.fori_loop(1, 8, give_share, 0)

    @pl.when(in_half == 1)
    def _():
        waiter(line_in.at[pl.ds(0, 15)], line_send, line_recv, here).wait()

    @pl.when(in_half == 0)
    def _():
        waiter(line_in, line_send, line_recv, here).wait()

    turned[...] = jnp.concatenate([add_up(line_in), jnp.zeros((80, 128), F32)], axis=0).T
    mine = turned[pl.ds(pl.multiple_of(64 * c, 64), 64), :]
    out_u[...] = mine[:, 0:32]
    out_o[...] = mine[:, 32:40]

    for half in range(2):
        waiter(share.at[half, pl.ds(0, 7)], share_send.at[half], share_recv.at[half], here).wait()
        for piece in range(8):
            out_table[32 * piece : 32 * piece + 32, 256 * half : 256 * half + 256] = share[half, piece].astype(F32)

    waiter(asked.at[most], ask_send, ask_recv, here).wait_send()
    for half in range(2):
        waiter(replies.at[half, most], reply_send.at[half], reply_recv.at[half], here).wait_send()

        @pl.when(is_source)
        def _(half=half):
            for step in range(4):
                waiter(shard.at[half], shard_send.at[half], shard_recv.at[half], here).wait_send()

        @pl.when(is_relay)
        def _(half=half):
            for step in range(2):
                waiter(shard.at[half], relay_send.at[half], shard_recv.at[half], here).wait_send()


def on_device(table, item_owner, item_row, lengths, cotangent, w_uvqk, w_out):
    vmem = pl.BlockSpec(memory_space=pltpu.VMEM)
    anywhere = pl.BlockSpec(memory_space=pl.ANY)
    dma = pltpu.SemaphoreType.DMA
    shape = jax.ShapeDtypeStruct

    def held(*sizes, kind=BF16):
        return pltpu.VMEM(sizes, kind)

    return pl.pallas_call(
        layer_kernel,
        out_shape=(shape((256, 512), F32), shape((64, 32), F32), shape((64, 8), F32)),
        in_specs=[anywhere] * 7,
        out_specs=(vmem,) * 3,
        scratch_shapes=[
            held(1, 128, kind=I32), held(1, 128, kind=I32), held(1, 6, kind=I32),
            held(128, 512), held(512, 2048), held(512, 512),
            held(2, 256, 256), held(64, 8, 128, kind=F32), held(64, 8, 128, kind=F32), held(512, 256),
            held(2, 64, 16, 128), held(2, 64, 16, 128),
            held(128, 2048, kind=F32), held(128, 2048), held(128, 2048, kind=F32),
            held(4, 2, 320, 512), held(2, 64, 16, 128), held(2, 64, 16, 128),
            held(4, 320, 512), held(4, 320, 512),
            held(4, 160, 512), held(4, 4, 160, 128), held(160, 512), held(4, 160, 128),
            held(4, 160, 128), held(4, 160, 128),
            held(8, 48, 128), held(16, 48, 128), held(2, 8, 32, 256), held(2, 8, 32, 256), held(2, 8, 32, 256),
            held(128, 128, kind=F32),
            dma((6,)), dma((2,)), dma((2,)), dma((2,)), dma, dma, dma((2,)), dma((2,)),
            dma((2,)), dma((2,)), dma((4,)), dma((4,)), dma((4,)), dma((4,)), dma, dma,
            dma((2,)), dma((2,)), dma((2,)), dma((2,)),
        ],
        compiler_params=pltpu.CompilerParams(collective_id=0, has_side_effects=True, vmem_limit_bytes=VMEM_LIMIT),
        name="layer",
    )(item_owner.reshape(1, 128), item_row.reshape(1, 128), lengths, table, cotangent, w_uvqk, w_out)


def solution(mesh):
    in_specs = (
        P("wide", None),
        P(("wide", "narrow"), None),
        P(("wide", "narrow")),
        P(("wide", "narrow"), None),
        P(("wide", "narrow"), None),
        P(),
        P(),
    )
    out_specs = (P("wide", None), P("narrow", "wide"), P("narrow", "wide"))
    return jax.shard_map(on_device, mesh=mesh, in_specs=in_specs, out_specs=out_specs, check_vma=False)
```

```python
import jax
import jax.numpy as jnp
from jax import lax
from jax.experimental import pallas as pl
from jax.experimental.pallas import tpu as pltpu
from jax.sharding import PartitionSpec as P

HEADS = 8
EPS = 1e-05
MESH = pl.DeviceIdType.MESH
F32, BF16, I32 = jnp.float32, jnp.bfloat16, jnp.int32
VMEM_LIMIT = 63 * 1024 * 1024


def div(value, by):
    return lax.div(value, jnp.int32(by))


def rem(value, by):
    return lax.rem(value, jnp.int32(by))


def coordinates():
    wide, narrow = lax.axis_index("wide"), lax.axis_index("narrow")
    return div(wide, 16), rem(wide, 16), div(narrow, 2), rem(narrow, 2)


def shard_z(y, c, b):
    return 2 * (rem(y + 2 * b, 4) + 4 * c) + 1 - b


def holder_of(z):
    b = 1 - rem(z, 2)
    half = div(z, 2)
    y = rem(rem(half, 4) + 4 - 2 * b, 4)
    return 2 * y + div(half, 4), b


def member(rank, a):
    narrow, b = holder_of(rem(rank, 16))
    return div(rank, 16) * 16 + 2 * a + b, narrow


def signal(sem, device):
    pl.semaphore_signal(sem, inc=1, device_id=device, device_id_type=MESH)


def send(src, dst, send_sem, recv_sem, device):
    pltpu.make_async_remote_copy(
        src_ref=src, dst_ref=dst, send_sem=send_sem, recv_sem=recv_sem, device_id=device, device_id_type=MESH
    ).start()


def waiter(ref, send_sem, recv_sem, device):
    return pltpu.make_async_remote_copy(
        src_ref=ref, dst_ref=ref, send_sem=send_sem, recv_sem=recv_sem, device_id=device, device_id_type=MESH
    )


def iota(shape, dim):
    return lax.broadcasted_iota(I32, shape, dim)


def onehot(hits):
    return jnp.where(hits, 1.0, 0.0).astype(BF16)


def dot(left, right, contract=((1,), (0,))):
    return lax.dot_general(left, right, (contract, ((), ())), preferred_element_type=F32)


def ranks(owner_t, owner_s):
    sub, lane = iota((128, 128), 0), iota((128, 128), 1)
    same = owner_t == owner_s
    across = jnp.sum(jnp.where(same & (sub < lane), 1.0, 0.0), axis=0, keepdims=True)
    down = jnp.sum(jnp.where(same & (lane < sub), 1.0, 0.0), axis=1, keepdims=True)
    return down, across


def to_blocks(first, second):
    return jnp.concatenate([first.reshape(64, 8, 128), second.reshape(64, 8, 128)], axis=1).astype(BF16)


def from_blocks(blocks):
    values = blocks.astype(F32)
    return jnp.concatenate([values[:, 0:8].reshape(512, 128), values[:, 8:16].reshape(512, 128)], axis=1).astype(BF16)


def mean_rows(values):
    return jnp.mean(values, axis=-1, keepdims=True)


def norm_back(grad, normed, scale):
    return scale * (grad - mean_rows(grad) - normed * mean_rows(grad * normed))


def weights_of_pairs(lengths):
    sub, lane = iota((128, 128), 0), iota((128, 128), 1)
    seg_t, seg_s = jnp.zeros((128, 128), I32), jnp.zeros((128, 128), I32)
    total = jnp.zeros((1, 1), I32)
    for i in range(6):
        total = total + lengths[0:1, i : i + 1]
        seg_t = seg_t + jnp.where(sub >= total, 1, 0)
        seg_s = seg_s + jnp.where(lane >= total, 1, 0)
    own_length = jnp.ones((128, 128), F32)
    for i in range(6):
        own_length = jnp.where(seg_t == i, lengths[0:1, i : i + 1].astype(F32), own_length)
    return jnp.where((seg_t == seg_s) & (lane <= sub), 1.0 / own_length, 0.0)


def layer_kernel(
    owner_hbm, row_hbm, lengths_hbm, table, cotangent_hbm, w_uvqk_hbm, w_out_hbm, shared, out_w,
    owner, row, lengths, cotangent, w_uvqk, w_out, shard, ask_out, asked, chosen, reply_out, replies,
    pre, act, grad_act, grad_pre, grads, rows_out, rows_in, pair_in, plane_out, x_in, y_in, x_mid, y_mid, xy_in, yx_in,
    line_out, line_in, sums, far_in, piece_out, piece_in, share,
    load_sem, shard_send, shard_recv, relay_send, ask_send, ask_recv, reply_send, reply_recv,
    rows_send, rows_recv, pair_send, pair_recv, plane_send, plane_recv, line_send, line_recv,
    far_send, far_recv, piece_send, piece_recv, share_send, share_recv, keep_sem,
):
    x, z, y, c = coordinates()
    wide = x * 16 + z
    a, b = div(z, 2), rem(z, 2)
    narrow = 2 * y + c
    here = (wide, narrow)
    my_z = shard_z(y, c, b)
    me = x * 16 + my_z
    to_narrow, to_b = holder_of(z)
    is_source = to_narrow == narrow
    away = rem(z - my_z + 16, 16)
    is_relay = jnp.logical_or(away == 3, away == 13)
    outward = jnp.where(away == 3, 1, -1)
    upper = div(z, 8)
    in_half = (upper == c).astype(I32)
    barrier = pltpu.get_barrier_semaphore()

    def on_line(at_z):
        return x * 16 + rem(at_z + 32, 16), narrow

    loads = []
    for i, (src, dst) in enumerate(
        [(owner_hbm, owner), (row_hbm, row), (lengths_hbm, lengths), (w_uvqk_hbm, w_uvqk), (cotangent_hbm, cotangent), (w_out_hbm, w_out)]
    ):
        loads.append(pltpu.make_async_copy(src, dst, load_sem.at[i]))
        loads[-1].start()

    parent = jnp.where(
        jnp.logical_or(away == 5, away == 7), my_z + 3, jnp.where(jnp.logical_or(away == 9, away == 11), my_z - 3, my_z)
    )
    signal(barrier, on_line(parent))

    def greet(step, carry):
        signal(barrier, member(rem(me + step, 64), a))
        return carry

    lax.fori_loop(1, 64, greet, 0)

    loads[0].wait()
    loads[1].wait()
    owner_s = jnp.broadcast_to(owner[...].astype(F32), (128, 128))
    owner_t = owner_s.T
    rank_t, rank_s = ranks(owner_t, owner_s)
    slot_s = (owner_s * 8.0 + rank_s)[0:1].astype(I32)
    slot_t = (owner_t * 16.0 + rank_t)[:, 0:1].astype(I32)
    slots = onehot(iota((512, 128), 0) == slot_s)
    named = (jnp.broadcast_to(row[...].astype(F32), (128, 128)).T + 1.0).astype(BF16)
    ask_out[...] = dot(slots, named).reshape(64, 8, 128)

    pl.semaphore_wait(barrier, 63 + 4 * is_source.astype(I32) + 2 * is_relay.astype(I32))

    @pl.when(is_source)
    def _():
        for steps in ((3, -3), (1, -1)):
            for half in range(2):
                for step in steps:
                    send(
                        table.at[:, pl.ds(256 * half, 256)], shard.at[half],
                        shard_send.at[half], shard_recv.at[half], on_line(z + step),
                    )

    def ask(step, carry):
        rank = rem(me + step, 64)
        send(ask_out.at[rank], asked.at[me], ask_send, ask_recv, member(rank, a))
        return carry

    lax.fori_loop(1, 64, ask, 0)
    asked[pl.ds(me, 1)] = ask_out[pl.ds(me, 1)]
    most = pl.ds(0, 63)

    @pl.when(is_relay)
    def _():
        for half in range(2):
            waiter(shard.at[half], shard_send.at[half], shard_recv.at[half], here).wait_recv()
            for step in (4, 2):
                send(
                    shard.at[half], shard.at[half],
                    relay_send.at[half], shard_recv.at[half], on_line(z + outward * step),
                )

    waiter(asked.at[most], ask_send, ask_recv, here).wait_recv()
    wanted = asked[...].reshape(512, 128).astype(I32)
    wanted = jnp.concatenate([wanted, wanted], axis=1)
    chosen[...] = onehot(wanted == iota((512, 256), 1) + 1)
    for half in range(2):
        @pl.when(jnp.logical_not(is_relay))
        def _(half=half):
            waiter(shard.at[half], shard_send.at[half], shard_recv.at[half], here).wait_recv()

        picked = dot(chosen[...], shard[half])
        reply_out[half] = to_blocks(picked[:, 0:128], picked[:, 128:256])

        def answer(step, carry, half=half):
            rank = rem(me + step, 64)
            send(
                reply_out.at[half, rank], replies.at[half, me],
                reply_send.at[half], reply_recv.at[half], member(rank, a),
            )
            return carry

        lax.fori_loop(1, 64, answer, 0)
        replies[half, pl.ds(me, 1)] = reply_out[half, pl.ds(me, 1)]

    loads[2].wait()
    weight = weights_of_pairs(lengths)
    spots = iota((128, 1024), 1)
    finds = (onehot(spots == slot_t), onehot(spots == slot_t + 8))
    parts = []
    for half in range(2):
        waiter(replies.at[half, most], reply_send.at[half], reply_recv.at[half], here).wait_recv()
        arrived = replies[half].reshape(1024, 128)
        parts += [dot(finds[0], arrived), dot(finds[1], arrived)]
    embedded = jnp.concatenate(parts, axis=1)
    center = embedded - mean_rows(embedded)
    embed_scale = lax.rsqrt(mean_rows(center * center) + EPS)
    embed_norm = center * embed_scale
    normed = embed_norm.astype(BF16)

    loads[3].wait()
    for part in range(4):
        cols = pl.ds(512 * part, 512)
        value = dot(normed, w_uvqk[:, cols])
        pre[:, cols] = value
        act[:, cols] = (value * jax.nn.sigmoid(value)).astype(BF16)

    first_half = iota((128, 128), 1) < 64
    keep = (first_half, jnp.logical_not(first_half))
    zero = jnp.zeros((128, 128), BF16)
    mixed = []
    for pair in range(4):
        q = act[:, 1024 + 128 * pair : 1152 + 128 * pair]
        k = act[:, 1536 + 128 * pair : 1664 + 128 * pair]
        v = act[:, 512 + 128 * pair : 640 + 128 * pair]
        both = jnp.zeros((128, 128), F32)
        for head in range(2):
            score = dot(jnp.where(keep[head], q, zero), k, ((1,), (1,))) * 0.125
            attention = (score * jax.nn.sigmoid(score) * weight).astype(BF16)
            both = both + dot(attention, jnp.where(keep[head], v, zero))
        mixed.append(both)
    mixture = jnp.concatenate(mixed, axis=1)
    center = mixture - mean_rows(mixture)
    mix_scale = lax.rsqrt(mean_rows(center * center) + EPS)
    mix_norm = center * mix_scale
    gate = act[:, 0:512].astype(F32)
    gated = (mix_norm * gate).astype(BF16)

    loads[4].wait()
    loads[5].wait()
    cot = cotangent[...]

    def back(part, grad_normed):
        cols = pl.ds(512 * part, 512)
        value = pre[:, cols]
        gain = jax.nn.sigmoid(value)
        grad_pre[:, cols] = (grad_act[:, cols] * (gain * (1.0 + value * (1.0 - gain)))).astype(BF16)
        return grad_normed + dot(grad_pre[:, cols], w_uvqk[:, cols], ((1,), (1,)))

    grad_gated = dot(cot, w_out[...], ((1,), (1,)))
    grad_act[:, 0:512] = grad_gated * mix_norm
    grad_normed = back(0, jnp.zeros((128, 512), F32))
    grad_mix = norm_back(grad_gated * gate, mix_norm, mix_scale).astype(BF16)
    for pair in range(4):
        q = act[:, 1024 + 128 * pair : 1152 + 128 * pair]
        k = act[:, 1536 + 128 * pair : 1664 + 128 * pair]
        v = act[:, 512 + 128 * pair : 640 + 128 * pair]
        g = grad_mix[:, 128 * pair : 128 * pair + 128]
        grad_q, grad_k, grad_v = [jnp.zeros((128, 128), F32)] * 3
        for head in range(2):
            q_one, k_one, v_one, g_one = [jnp.where(keep[head], part, zero) for part in (q, k, v, g)]
            score = dot(q_one, k, ((1,), (1,))) * 0.125
            gain = jax.nn.sigmoid(score)
            attention = (score * gain * weight).astype(BF16)
            grad_att = dot(g_one, v, ((1,), (1,)))
            grad_score = (grad_att * weight * (gain * (1.0 + score * (1.0 - gain))) * 0.125).astype(BF16)
            grad_v = grad_v + dot(attention, g_one, ((0,), (0,)))
            grad_q = grad_q + dot(grad_score, k_one)
            grad_k = grad_k + dot(grad_score, q_one, ((0,), (0,)))
        grad_act[:, 512 + 128 * pair : 640 + 128 * pair] = grad_v
        grad_act[:, 1024 + 128 * pair : 1152 + 128 * pair] = grad_q
        grad_act[:, 1536 + 128 * pair : 1664 + 128 * pair] = grad_k
    for part in range(1, 4):
        grad_normed = back(part, grad_normed)
    grad_embed = (cot.astype(F32) + norm_back(grad_normed, embed_norm, embed_scale)).astype(BF16)

    def give_rows(half):
        given = dot(slots, grad_embed[:, 256 * half : 256 * half + 256])
        rows_out[half] = to_blocks(given[:, 0:128], given[:, 128:256])

        def give(step, carry):
            rank = rem(me + step, 64)
            send(
                rows_out.at[half, rank], rows_in.at[half, me],
                rows_send.at[half], rows_recv.at[half], member(rank, a),
            )
            return carry

        lax.fori_loop(1, 64, give, 0)
        rows_in[half, pl.ds(me, 1)] = rows_out[half, pl.ds(me, 1)]

    give_rows(0)
    give_rows(1)

    grad_o = dot(cot, gated, ((0,), (0,))).astype(BF16)
    partner = (wide, 2 * y + 1 - c)
    for part in range(4):
        grad_u = dot(grad_pre[:, pl.ds(512 * part, 512)], normed, ((0,), (0,))).astype(BF16)
        for side in range(2):
            grads[part, side, 0:256] = grad_u[256 * side : 256 * side + 256]
            grads[part, side, 256:320] = grad_o[128 * part + 64 * side : 128 * part + 64 * side + 64]
        send(grads.at[part, 1 - c], pair_in.at[part], pair_send.at[part], pair_recv.at[part], partner)
    for part in range(4):
        waiter(pair_in.at[part], pair_send.at[part], pair_recv.at[part], here).wait()
        mine = grads[part, pl.ds(c, 1)].reshape(320, 512).astype(F32)
        plane_out[part] = (mine + pair_in[part].astype(F32)).astype(BF16)
    for step in range(1, 4):
        to_x, to_y = rem(x + step, 4), rem(y + step, 4)
        send(
            plane_out.at[to_x, pl.ds(0, 160)], x_in.at[x], plane_send.at[0], plane_recv.at[0],
            (to_x * 16 + z, narrow),
        )
        send(
            plane_out.at[:, pl.ds(160, 160), pl.ds(pl.multiple_of(128 * to_y, 128), 128)], y_in.at[y],
            plane_send.at[1], plane_recv.at[1], (wide, 2 * to_y + c),
        )
    my_lanes = pl.ds(pl.multiple_of(128 * y, 128), 128)
    x_in[pl.ds(x, 1)] = plane_out[pl.ds(x, 1), 0:160]
    y_in[pl.ds(y, 1)] = plane_out[:, 160:320, my_lanes].reshape(1, 4, 160, 128)

    is_far = jnp.logical_and(away >= 5, away <= 11)
    child = jnp.logical_or(away == 7, away == 9).astype(I32)
    place = jnp.where(away == 1, 0, jnp.where(away == 3, 1, jnp.where(away == 13, 2, 3)))

    def give_pieces(half):
        def give(step, carry):
            to = rem(narrow + step, 8)
            send(
                piece_out.at[half, pl.ds(pl.multiple_of(32 * to, 32), 32)], piece_in.at[half, place],
                piece_send.at[half], piece_recv.at[half], (x * 16 + my_z, to),
            )
            return carry

        lax.fori_loop(0, 8, give, 0)

    for half in range(2):
        waiter(rows_in.at[half, most], rows_send.at[half], rows_recv.at[half], here).wait()
        sums[half] = dot(chosen[...], from_blocks(rows_in[half]), ((0,), (0,)))

        @pl.when(jnp.logical_not(is_relay))
        def _(half=half):
            piece_out[half] = sums[half].astype(BF16)

            @pl.when(is_far)
            def _():
                send(piece_out.at[half], far_in.at[half, child], far_send.at[half], far_recv.at[half], on_line(parent))

            @pl.when(jnp.logical_not(is_far))
            def _():
                give_pieces(half)

    @pl.when(is_relay)
    def _():
        for half in range(2):
            waiter(far_in.at[half], far_send.at[half], far_recv.at[half], here).wait_recv()
            total = sums[half] + far_in[half, 0].astype(F32) + far_in[half, 1].astype(F32)
            piece_out[half] = total.astype(BF16)
            give_pieces(half)

    three = pl.ds(0, 3)

    def add_up(ref):
        total = ref[0].astype(F32)
        for step in range(1, ref.shape[0]):
            total = total + ref[step].astype(F32)
        return total

    waiter(x_in.at[three], plane_send.at[0], plane_recv.at[0], here).wait()
    x_mid[...] = add_up(x_in).astype(BF16)
    for step in range(1, 4):
        to_y = rem(y + step, 4)
        send(
            x_mid.at[:, pl.ds(pl.multiple_of(128 * to_y, 128), 128)], xy_in.at[y],
            plane_send.at[2], plane_recv.at[2], (wide, 2 * to_y + c),
        )
    xy_in[pl.ds(y, 1)] = x_mid[:, my_lanes].reshape(1, 160, 128)
    waiter(y_in.at[three], plane_send.at[1], plane_recv.at[1], here).wait()
    y_mid[...] = add_up(y_in).astype(BF16)
    for step in range(1, 4):
        to_x = rem(x + step, 4)
        send(y_mid.at[to_x], yx_in.at[x], plane_send.at[3], plane_recv.at[3], (to_x * 16 + z, narrow))
    yx_in[pl.ds(x, 1)] = y_mid[pl.ds(x, 1)]
    waiter(xy_in.at[three], plane_send.at[2], plane_recv.at[2], here).wait()
    waiter(yx_in.at[three], plane_send.at[3], plane_recv.at[3], here).wait()
    total = jnp.concatenate([add_up(xy_in), add_up(yx_in)], axis=0)
    for step in range(8):
        line_out[step] = jnp.concatenate(
            [total[32 * step : 32 * step + 32], total[256 + 8 * step : 264 + 8 * step], jnp.zeros((8, 128), F32)], axis=0
        ).astype(BF16)

    def give_line(step, carry):
        to_z = 8 * c + step
        for core in range(2):
            own = jnp.logical_and(to_z == z, c == core)

            @pl.when(jnp.logical_not(own))
            def _():
                send(line_out.at[step], line_in.at[z], line_send, line_recv, (x * 16 + to_z, 2 * y + core))

            @pl.when(own)
            def _():
                line_in[pl.ds(z, 1)] = line_out[pl.ds(step, 1)]

        return carry

    lax.fori_loop(0, 8, give_line, 0)

    keeps = []
    for half in range(2):
        waiter(piece_in.at[half], piece_send.at[half], piece_recv.at[half], here).wait_recv()
        share[half] = add_up(piece_in.at[half]).astype(BF16)
        keeps.append(pltpu.make_async_copy(share.at[half], shared.at[half, narrow], keep_sem.at[half]))
        keeps[-1].start()

        def give_share(step, carry, half=half):
            send(
                share.at[half], shared.at[half, narrow],
                share_send.at[half], share_recv.at[half], (wide, rem(narrow + step, 8)),
            )
            return carry

        lax.fori_loop(1, 8, give_share, 0)

    @pl.when(in_half == 1)
    def _():
        waiter(line_in.at[pl.ds(0, 15)], line_send, line_recv, here).wait()

    @pl.when(in_half == 0)
    def _():
        waiter(line_in, line_send, line_recv, here).wait()

    total = add_up(line_in)
    out_w[...] = jnp.where(c == 0, total[0:40, 0:64], total[0:40, 64:128])

    waiter(asked.at[most], ask_send, ask_recv, here).wait_send()
    for half in range(2):
        waiter(replies.at[half, most], reply_send.at[half], reply_recv.at[half], here).wait_send()

        @pl.when(is_source)
        def _(half=half):
            for step in range(4):
                waiter(shard.at[half], shard_send.at[half], shard_recv.at[half], here).wait_send()

        @pl.when(is_relay)
        def _(half=half):
            for step in range(2):
                waiter(shard.at[half], relay_send.at[half], shard_recv.at[half], here).wait_send()

        @pl.when(is_far)
        def _(half=half):
            waiter(piece_out.at[half], far_send.at[half], far_recv.at[half], here).wait_send()

        @pl.when(jnp.logical_not(is_far))
        def _(half=half):
            waiter(piece_out.at[half], piece_send.at[half], piece_recv.at[half], here).wait_send()

    for half in range(2):
        waiter(shared.at[half, pl.ds(0, 7)], share_send.at[half], share_recv.at[half], here).wait()
        keeps[half].wait()


def finish_kernel(shared, sums, out_table, out_u, out_o):
    for half in range(2):
        out_table[:, 256 * half : 256 * half + 256] = shared[half].reshape(256, 256).astype(F32)
    out_u[...] = sums[0:32]
    out_o[...] = sums[32:40]


def on_device(table, item_owner, item_row, lengths, cotangent, w_uvqk, w_out):
    vmem = pl.BlockSpec(memory_space=pltpu.VMEM)
    anywhere = pl.BlockSpec(memory_space=pl.ANY)
    dma = pltpu.SemaphoreType.DMA
    shape = jax.ShapeDtypeStruct

    def held(*sizes, kind=BF16):
        return pltpu.VMEM(sizes, kind)

    shared, sums = pl.pallas_call(
        layer_kernel,
        out_shape=(shape((2, 8, 32, 256), BF16), shape((40, 64), F32)),
        in_specs=[anywhere] * 7,
        out_specs=(anywhere, vmem),
        scratch_shapes=[
            held(1, 128, kind=I32), held(1, 128, kind=I32), held(1, 6, kind=I32),
            held(128, 512), held(512, 2048), held(512, 512),
            held(2, 256, 256), held(64, 8, 128, kind=F32), held(64, 8, 128, kind=F32), held(512, 256),
            held(2, 64, 16, 128), held(2, 64, 16, 128),
            held(128, 2048, kind=F32), held(128, 2048), held(128, 2048, kind=F32), held(128, 2048),
            held(4, 2, 320, 512), held(2, 64, 16, 128), held(2, 64, 16, 128),
            held(4, 320, 512), held(4, 320, 512),
            held(4, 160, 512), held(4, 4, 160, 128), held(160, 512), held(4, 160, 128),
            held(4, 160, 128), held(4, 160, 128),
            held(8, 48, 128), held(16, 48, 128),
            held(2, 256, 256, kind=F32), held(2, 2, 256, 256), held(2, 256, 256), held(2, 4, 32, 256), held(2, 32, 256),
            dma((6,)), dma((2,)), dma((2,)), dma((2,)), dma, dma, dma((2,)), dma((2,)),
            dma((2,)), dma((2,)), dma((4,)), dma((4,)), dma((4,)), dma((4,)), dma, dma,
            dma((2,)), dma((2,)), dma((2,)), dma((2,)), dma((2,)), dma((2,)), dma((2,)),
        ],
        compiler_params=pltpu.CompilerParams(collective_id=0, has_side_effects=True, vmem_limit_bytes=VMEM_LIMIT),
        name="layer",
    )(item_owner.reshape(1, 128), item_row.reshape(1, 128), lengths, table, cotangent, w_uvqk, w_out)

    grad_table, grad_uvqk, grad_out = pl.pallas_call(
        finish_kernel,
        out_shape=(shape((256, 512), F32), shape((32, 64), F32), shape((8, 64), F32)),
        in_specs=[vmem] * 2,
        out_specs=(vmem,) * 3,
        name="finish",
    )(shared, sums)
    return grad_table, grad_uvqk.T, grad_out.T


def solution(mesh):
    in_specs = (
        P("wide", None),
        P(("wide", "narrow"), None),
        P(("wide", "narrow")),
        P(("wide", "narrow"), None),
        P(("wide", "narrow"), None),
        P(),
        P(),
    )
    out_specs = (P("wide", None), P("narrow", "wide"), P("narrow", "wide"))
    return jax.shard_map(on_device, mesh=mesh, in_specs=in_specs, out_specs=out_specs, check_vma=False)
```

```python
import jax
import jax.numpy as jnp
from jax import lax
from jax.experimental import pallas as pl
from jax.experimental.pallas import tpu as pltpu
from jax.sharding import PartitionSpec as P

HEADS = 8
EPS = 1e-05
MESH = pl.DeviceIdType.MESH
F32, BF16, I32 = jnp.float32, jnp.bfloat16, jnp.int32
VMEM_LIMIT = 63 * 1024 * 1024


def div(value, by):
    return lax.div(value, jnp.int32(by))


def rem(value, by):
    return lax.rem(value, jnp.int32(by))


def coordinates():
    wide, narrow = lax.axis_index("wide"), lax.axis_index("narrow")
    return div(wide, 16), rem(wide, 16), div(narrow, 2), rem(narrow, 2)


def shard_z(y, c, b):
    return 2 * (rem(y + 2 * b, 4) + 4 * c) + 1 - b


def holder_of(z):
    b = 1 - rem(z, 2)
    half = div(z, 2)
    y = rem(rem(half, 4) + 4 - 2 * b, 4)
    return 2 * y + div(half, 4), b


def member(rank, a):
    narrow, b = holder_of(rem(rank, 16))
    return div(rank, 16) * 16 + 2 * a + b, narrow


def signal(sem, device):
    pl.semaphore_signal(sem, inc=1, device_id=device, device_id_type=MESH)


def send(src, dst, send_sem, recv_sem, device):
    pltpu.make_async_remote_copy(
        src_ref=src, dst_ref=dst, send_sem=send_sem, recv_sem=recv_sem, device_id=device, device_id_type=MESH
    ).start()


def waiter(ref, send_sem, recv_sem, device):
    return pltpu.make_async_remote_copy(
        src_ref=ref, dst_ref=ref, send_sem=send_sem, recv_sem=recv_sem, device_id=device, device_id_type=MESH
    )


def iota(shape, dim):
    return lax.broadcasted_iota(I32, shape, dim)


def onehot(hits):
    return jnp.where(hits, 1.0, 0.0).astype(BF16)


def dot(left, right, contract=((1,), (0,))):
    return lax.dot_general(left, right, (contract, ((), ())), preferred_element_type=F32)


def ranks(owner_t, owner_s):
    sub, lane = iota((128, 128), 0), iota((128, 128), 1)
    same = owner_t == owner_s
    across = jnp.sum(jnp.where(same & (sub < lane), 1.0, 0.0), axis=0, keepdims=True)
    down = jnp.sum(jnp.where(same & (lane < sub), 1.0, 0.0), axis=1, keepdims=True)
    return down, across


def to_blocks(first, second, lanes):
    return jnp.concatenate([first.reshape(64, 8, lanes), second.reshape(64, 8, lanes)], axis=1).astype(BF16)


def mean_rows(values):
    return jnp.mean(values, axis=-1, keepdims=True)


def norm_back(grad, normed, scale):
    return scale * (grad - mean_rows(grad) - normed * mean_rows(grad * normed))


def weights_of_pairs(lengths):
    sub, lane = iota((128, 128), 0), iota((128, 128), 1)
    seg_t, seg_s = jnp.zeros((128, 128), I32), jnp.zeros((128, 128), I32)
    total = jnp.zeros((1, 1), I32)
    for i in range(6):
        total = total + lengths[0:1, i : i + 1]
        seg_t = seg_t + jnp.where(sub >= total, 1, 0)
        seg_s = seg_s + jnp.where(lane >= total, 1, 0)
    own_length = jnp.ones((128, 128), F32)
    for i in range(6):
        own_length = jnp.where(seg_t == i, lengths[0:1, i : i + 1].astype(F32), own_length)
    return jnp.where((seg_t == seg_s) & (lane <= sub), 1.0 / own_length, 0.0)


def layer_kernel(
    owner_hbm, row_hbm, lengths_hbm, table, cotangent_hbm, w_uvqk_hbm, w_out_hbm, shared, out_w,
    owner, row, lengths, cotangent, w_uvqk, w_out, shard, ask_out, asked, chosen, reply_out, replies,
    pre, act, grad_act, grad_pre, grads, rows_out, rows_in, pair_in, plane_out, x_in, y_in, x_mid, y_mid, xy_in, yx_in,
    line_out, line_in, sums, chain_in, chain_out, piece_in, share,
    load_sem, shard_send, shard_recv, pass_send, ask_send, ask_recv, reply_send, reply_recv,
    rows_send, rows_recv, pair_send, pair_recv, plane_send, plane_recv, line_send, line_recv,
    chain_send, chain_recv, piece_recv, share_send, share_recv, keep_sem,
):
    x, z, y, c = coordinates()
    wide = x * 16 + z
    a, b = div(z, 2), rem(z, 2)
    narrow = 2 * y + c
    here = (wide, narrow)
    my_z = shard_z(y, c, b)
    me = x * 16 + my_z
    to_narrow, to_b = holder_of(z)
    is_source = to_narrow == narrow
    away = rem(z - my_z + 16, 16)
    outward = jnp.where(away < 8, 1, -1)
    hops = jnp.where(away < 8, away, 16 - away)
    passes_on = hops < 7
    upper = div(z, 8)
    in_half = (upper == c).astype(I32)
    barrier = pltpu.get_barrier_semaphore()

    def on_line(at_z):
        return x * 16 + rem(at_z + 32, 16), narrow

    loads = []
    for i, (src, dst) in enumerate(
        [(owner_hbm, owner), (row_hbm, row), (lengths_hbm, lengths), (w_uvqk_hbm, w_uvqk), (cotangent_hbm, cotangent), (w_out_hbm, w_out)]
    ):
        loads.append(pltpu.make_async_copy(src, dst, load_sem.at[i]))
        loads[-1].start()

    parent = jnp.where(hops == 1, my_z, z - 2 * outward)
    signal(barrier, on_line(parent))

    def greet(step, carry):
        signal(barrier, member(rem(me + step, 64), a))
        return carry

    lax.fori_loop(1, 64, greet, 0)

    loads[0].wait()
    loads[1].wait()
    owner_s = jnp.broadcast_to(owner[...].astype(F32), (128, 128))
    owner_t = owner_s.T
    rank_t, rank_s = ranks(owner_t, owner_s)
    slot_s = (owner_s * 8.0 + rank_s)[0:1].astype(I32)
    slot_t = (owner_t * 16.0 + rank_t)[:, 0:1].astype(I32)
    slots = onehot(iota((512, 128), 0) == slot_s)
    named = (jnp.broadcast_to(row[...].astype(F32), (128, 128)).T + 1.0).astype(BF16)
    ask_out[...] = dot(slots, named).reshape(64, 8, 128)

    pl.semaphore_wait(barrier, 63 + 2 * is_source.astype(I32) + passes_on.astype(I32))

    @pl.when(is_source)
    def _():
        for piece in range(4):
            for step in (1, -1):
                send(
                    table.at[:, pl.ds(128 * piece, 128)], shard.at[piece],
                    shard_send.at[piece], shard_recv.at[piece], on_line(z + step),
                )

    def ask(step, carry):
        rank = rem(me + step, 64)
        send(ask_out.at[rank], asked.at[me], ask_send, ask_recv, member(rank, a))
        return carry

    lax.fori_loop(1, 64, ask, 0)
    asked[pl.ds(me, 1)] = ask_out[pl.ds(me, 1)]
    most = pl.ds(0, 63)

    @pl.when(passes_on)
    def _():
        for piece in range(4):
            waiter(shard.at[piece], shard_send.at[piece], shard_recv.at[piece], here).wait_recv()
            send(
                shard.at[piece], shard.at[piece],
                pass_send.at[piece], shard_recv.at[piece], on_line(z + 2 * outward),
            )

    waiter(asked.at[most], ask_send, ask_recv, here).wait_recv()
    wanted = asked[...].reshape(512, 128).astype(I32)
    wanted = jnp.concatenate([wanted, wanted], axis=1)
    chosen[...] = onehot(wanted == iota((512, 256), 1) + 1)
    for half in range(2):
        @pl.when(jnp.logical_not(passes_on))
        def _(half=half):
            for piece in (2 * half, 2 * half + 1):
                waiter(shard.at[piece], shard_send.at[piece], shard_recv.at[piece], here).wait_recv()

        picked = dot(chosen[...], jnp.concatenate([shard[2 * half], shard[2 * half + 1]], axis=1))
        reply_out[half] = to_blocks(picked[:, 0:128], picked[:, 128:256], 128)

        def answer(step, carry, half=half):
            rank = rem(me + step, 64)
            send(
                reply_out.at[half, rank], replies.at[half, me],
                reply_send.at[half], reply_recv.at[half], member(rank, a),
            )
            return carry

        lax.fori_loop(1, 64, answer, 0)
        replies[half, pl.ds(me, 1)] = reply_out[half, pl.ds(me, 1)]

    loads[2].wait()
    weight = weights_of_pairs(lengths)
    spots = iota((128, 1024), 1)
    finds = (onehot(spots == slot_t), onehot(spots == slot_t + 8))
    parts = []
    for half in range(2):
        waiter(replies.at[half, most], reply_send.at[half], reply_recv.at[half], here).wait_recv()
        arrived = replies[half].reshape(1024, 128)
        parts += [dot(finds[0], arrived), dot(finds[1], arrived)]
    embedded = jnp.concatenate(parts, axis=1)
    center = embedded - mean_rows(embedded)
    embed_scale = lax.rsqrt(mean_rows(center * center) + EPS)
    embed_norm = center * embed_scale
    normed = embed_norm.astype(BF16)

    loads[3].wait()
    for part in range(4):
        cols = pl.ds(512 * part, 512)
        value = dot(normed, w_uvqk[:, cols])
        pre[:, cols] = value
        act[:, cols] = (value * jax.nn.sigmoid(value)).astype(BF16)

    first_half = iota((128, 128), 1) < 64
    keep = (first_half, jnp.logical_not(first_half))
    zero = jnp.zeros((128, 128), BF16)
    mixed = []
    for pair in range(4):
        q = act[:, 1024 + 128 * pair : 1152 + 128 * pair]
        k = act[:, 1536 + 128 * pair : 1664 + 128 * pair]
        v = act[:, 512 + 128 * pair : 640 + 128 * pair]
        both = jnp.zeros((128, 128), F32)
        for head in range(2):
            score = dot(jnp.where(keep[head], q, zero), k, ((1,), (1,))) * 0.125
            attention = (score * jax.nn.sigmoid(score) * weight).astype(BF16)
            both = both + dot(attention, jnp.where(keep[head], v, zero))
        mixed.append(both)
    mixture = jnp.concatenate(mixed, axis=1)
    center = mixture - mean_rows(mixture)
    mix_scale = lax.rsqrt(mean_rows(center * center) + EPS)
    mix_norm = center * mix_scale
    gate = act[:, 0:512].astype(F32)
    gated = (mix_norm * gate).astype(BF16)

    loads[4].wait()
    loads[5].wait()
    cot = cotangent[...]

    def back(part, grad_normed):
        cols = pl.ds(512 * part, 512)
        value = pre[:, cols]
        gain = jax.nn.sigmoid(value)
        grad_pre[:, cols] = (grad_act[:, cols] * (gain * (1.0 + value * (1.0 - gain)))).astype(BF16)
        return grad_normed + dot(grad_pre[:, cols], w_uvqk[:, cols], ((1,), (1,)))

    grad_gated = dot(cot, w_out[...], ((1,), (1,)))
    grad_act[:, 0:512] = grad_gated * mix_norm
    grad_normed = back(0, jnp.zeros((128, 512), F32))
    grad_mix = norm_back(grad_gated * gate, mix_norm, mix_scale).astype(BF16)
    for pair in range(4):
        q = act[:, 1024 + 128 * pair : 1152 + 128 * pair]
        k = act[:, 1536 + 128 * pair : 1664 + 128 * pair]
        v = act[:, 512 + 128 * pair : 640 + 128 * pair]
        g = grad_mix[:, 128 * pair : 128 * pair + 128]
        grad_q, grad_k, grad_v = [jnp.zeros((128, 128), F32)] * 3
        for head in range(2):
            q_one, k_one, v_one, g_one = [jnp.where(keep[head], part, zero) for part in (q, k, v, g)]
            score = dot(q_one, k, ((1,), (1,))) * 0.125
            gain = jax.nn.sigmoid(score)
            attention = (score * gain * weight).astype(BF16)
            grad_att = dot(g_one, v, ((1,), (1,)))
            grad_score = (grad_att * weight * (gain * (1.0 + score * (1.0 - gain))) * 0.125).astype(BF16)
            grad_v = grad_v + dot(attention, g_one, ((0,), (0,)))
            grad_q = grad_q + dot(grad_score, k_one)
            grad_k = grad_k + dot(grad_score, q_one, ((0,), (0,)))
        grad_act[:, 512 + 128 * pair : 640 + 128 * pair] = grad_v
        grad_act[:, 1024 + 128 * pair : 1152 + 128 * pair] = grad_q
        grad_act[:, 1536 + 128 * pair : 1664 + 128 * pair] = grad_k
    for part in range(1, 4):
        grad_normed = back(part, grad_normed)
    grad_embed = (cot.astype(F32) + norm_back(grad_normed, embed_norm, embed_scale)).astype(BF16)

    given = dot(slots, grad_embed)
    rows_out[...] = to_blocks(given[:, 0:256], given[:, 256:512], 256)

    def give_rows(step, carry):
        rank = rem(me + step, 64)
        send(rows_out.at[rank], rows_in.at[me], rows_send, rows_recv, member(rank, a))
        return carry

    lax.fori_loop(1, 64, give_rows, 0)
    rows_in[pl.ds(me, 1)] = rows_out[pl.ds(me, 1)]

    grad_o = dot(cot, gated, ((0,), (0,))).astype(BF16)
    partner = (wide, 2 * y + 1 - c)
    for part in range(4):
        grad_u = dot(grad_pre[:, pl.ds(512 * part, 512)], normed, ((0,), (0,))).astype(BF16)
        for side in range(2):
            grads[part, side, 0:256] = grad_u[256 * side : 256 * side + 256]
            grads[part, side, 256:320] = grad_o[128 * part + 64 * side : 128 * part + 64 * side + 64]
        send(grads.at[part, 1 - c], pair_in.at[part], pair_send.at[part], pair_recv.at[part], partner)
    for part in range(4):
        waiter(pair_in.at[part], pair_send.at[part], pair_recv.at[part], here).wait()
        mine = grads[part, pl.ds(c, 1)].reshape(320, 512).astype(F32)
        plane_out[part] = (mine + pair_in[part].astype(F32)).astype(BF16)
    for step in range(1, 4):
        to_x, to_y = rem(x + step, 4), rem(y + step, 4)
        send(
            plane_out.at[to_x, pl.ds(0, 160)], x_in.at[x], plane_send.at[0], plane_recv.at[0],
            (to_x * 16 + z, narrow),
        )
        send(
            plane_out.at[:, pl.ds(160, 160), pl.ds(pl.multiple_of(128 * to_y, 128), 128)], y_in.at[y],
            plane_send.at[1], plane_recv.at[1], (wide, 2 * to_y + c),
        )
    my_lanes = pl.ds(pl.multiple_of(128 * y, 128), 128)
    x_in[pl.ds(x, 1)] = plane_out[pl.ds(x, 1), 0:160]
    y_in[pl.ds(y, 1)] = plane_out[:, 160:320, my_lanes].reshape(1, 4, 160, 128)

    waiter(rows_in.at[most], rows_send, rows_recv, here).wait()
    arrived = rows_in[...].astype(F32)
    for half in range(2):
        sums[half] = dot(chosen[...], arrived[:, 8 * half : 8 * half + 8].reshape(512, 256).astype(BF16), ((0,), (0,)))

    def pass_sums():
        for piece in range(4):
            mine = sums[piece // 2, :, 128 * (piece % 2) : 128 * (piece % 2) + 128]
            chain_out[piece] = mine.astype(BF16)

            @pl.when(passes_on)
            def _(piece=piece, mine=mine):
                waiter(chain_in.at[piece], chain_send.at[piece], chain_recv.at[piece], here).wait_recv()
                chain_out[piece] = (mine + chain_in[piece].astype(F32)).astype(BF16)

            @pl.when(hops > 1)
            def _(piece=piece):
                send(
                    chain_out.at[piece], chain_in.at[piece],
                    chain_send.at[piece], chain_recv.at[piece], on_line(parent),
                )

            @pl.when(hops == 1)
            def _(piece=piece):
                for to in range(8):
                    send(
                        chain_out.at[piece, pl.ds(32 * to, 32)], piece_in.at[piece, div(1 - outward, 2)],
                        chain_send.at[piece], piece_recv.at[piece], (x * 16 + my_z, to),
                    )

    @pl.when(hops > 1)
    def _():
        pass_sums()

    three = pl.ds(0, 3)

    def add_up(ref):
        total = ref[0].astype(F32)
        for step in range(1, ref.shape[0]):
            total = total + ref[step].astype(F32)
        return total

    waiter(x_in.at[three], plane_send.at[0], plane_recv.at[0], here).wait()
    x_mid[...] = add_up(x_in).astype(BF16)
    for step in range(1, 4):
        to_y = rem(y + step, 4)
        send(
            x_mid.at[:, pl.ds(pl.multiple_of(128 * to_y, 128), 128)], xy_in.at[y],
            plane_send.at[2], plane_recv.at[2], (wide, 2 * to_y + c),
        )
    xy_in[pl.ds(y, 1)] = x_mid[:, my_lanes].reshape(1, 160, 128)
    waiter(y_in.at[three], plane_send.at[1], plane_recv.at[1], here).wait()
    y_mid[...] = add_up(y_in).astype(BF16)
    for step in range(1, 4):
        to_x = rem(x + step, 4)
        send(y_mid.at[to_x], yx_in.at[x], plane_send.at[3], plane_recv.at[3], (to_x * 16 + z, narrow))
    yx_in[pl.ds(x, 1)] = y_mid[pl.ds(x, 1)]
    @pl.when(hops == 1)
    def _():
        pass_sums()

    waiter(xy_in.at[three], plane_send.at[2], plane_recv.at[2], here).wait()
    waiter(yx_in.at[three], plane_send.at[3], plane_recv.at[3], here).wait()
    total = jnp.concatenate([add_up(xy_in), add_up(yx_in)], axis=0)
    rolled = pltpu.roll(total, 64, 1)
    left = iota((16, 128), 1) < 64
    for step in range(8):
        top, bottom = slice(32 * step, 32 * step + 16), slice(32 * step + 16, 32 * step + 32)
        rest = slice(256 + 8 * step, 264 + 8 * step)
        first = jnp.where(left, total[top], rolled[bottom])
        second = jnp.where(left, rolled[top], total[bottom])
        for core, packed, values in ((0, first, total), (1, second, rolled)):
            line_out[step, core] = jnp.concatenate([packed, values[rest], jnp.zeros((8, 128), F32)], axis=0).astype(BF16)

    def give_line(step, carry):
        to_z = 8 * c + step
        for core in range(2):
            own = jnp.logical_and(to_z == z, c == core)

            @pl.when(jnp.logical_not(own))
            def _():
                send(line_out.at[step, core], line_in.at[z], line_send, line_recv, (x * 16 + to_z, 2 * y + core))

            @pl.when(own)
            def _():
                line_in[pl.ds(z, 1)] = line_out[pl.ds(step, 1), core]

        return carry

    lax.fori_loop(0, 8, give_line, 0)

    keeps = []
    for half in range(2):
        quarters = []
        for piece in (2 * half, 2 * half + 1):
            waiter(piece_in.at[piece], chain_send.at[piece], piece_recv.at[piece], here).wait_recv()
            quarters.append(add_up(piece_in.at[piece]))
        share[half] = jnp.concatenate(quarters, axis=1).astype(BF16)
        keeps.append(pltpu.make_async_copy(share.at[half], shared.at[half, narrow], keep_sem.at[half]))
        keeps[-1].start()

        def give_share(step, carry, half=half):
            send(
                share.at[half], shared.at[half, narrow],
                share_send.at[half], share_recv.at[half], (wide, rem(narrow + step, 8)),
            )
            return carry

        lax.fori_loop(1, 8, give_share, 0)

    @pl.when(in_half == 1)
    def _():
        waiter(line_in.at[pl.ds(0, 15)], line_send, line_recv, here).wait()

    @pl.when(in_half == 0)
    def _():
        waiter(line_in, line_send, line_recv, here).wait()

    total = add_up(line_in)
    out_w[0:16] = total[0:16, 0:64]
    out_w[16:32] = total[0:16, 64:128]
    out_w[32:40] = total[16:24, 0:64]

    waiter(asked.at[most], ask_send, ask_recv, here).wait_send()
    for half in range(2):
        waiter(replies.at[half, most], reply_send.at[half], reply_recv.at[half], here).wait_send()

    for piece in range(4):

        @pl.when(is_source)
        def _(piece=piece):
            for step in range(2):
                waiter(shard.at[piece], shard_send.at[piece], shard_recv.at[piece], here).wait_send()

        @pl.when(passes_on)
        def _(piece=piece):
            waiter(shard.at[piece], pass_send.at[piece], shard_recv.at[piece], here).wait_send()

        waiter(chain_out.at[piece], chain_send.at[piece], chain_recv.at[piece], here).wait_send()

    for half in range(2):
        waiter(shared.at[half, pl.ds(0, 7)], share_send.at[half], share_recv.at[half], here).wait()
        keeps[half].wait()


def finish_kernel(shared, sums, out_table, out_u, out_o):
    for half in range(2):
        out_table[:, 256 * half : 256 * half + 256] = shared[half].reshape(256, 256).astype(F32)
    out_u[...] = sums[0:32]
    out_o[...] = sums[32:40]


def on_device(table, item_owner, item_row, lengths, cotangent, w_uvqk, w_out):
    vmem = pl.BlockSpec(memory_space=pltpu.VMEM)
    anywhere = pl.BlockSpec(memory_space=pl.ANY)
    dma = pltpu.SemaphoreType.DMA
    shape = jax.ShapeDtypeStruct

    def held(*sizes, kind=BF16):
        return pltpu.VMEM(sizes, kind)

    shared, sums = pl.pallas_call(
        layer_kernel,
        out_shape=(shape((2, 8, 32, 256), BF16), shape((40, 64), F32)),
        in_specs=[anywhere] * 7,
        out_specs=(anywhere, vmem),
        scratch_shapes=[
            held(1, 128, kind=I32), held(1, 128, kind=I32), held(1, 6, kind=I32),
            held(128, 512), held(512, 2048), held(512, 512),
            held(4, 256, 128), held(64, 8, 128, kind=F32), held(64, 8, 128, kind=F32), held(512, 256),
            held(2, 64, 16, 128), held(2, 64, 16, 128),
            held(128, 2048, kind=F32), held(128, 2048), held(128, 2048, kind=F32), held(128, 2048),
            held(4, 2, 320, 512), held(64, 16, 256), held(64, 16, 256),
            held(4, 320, 512), held(4, 320, 512),
            held(4, 160, 512), held(4, 4, 160, 128), held(160, 512), held(4, 160, 128),
            held(4, 160, 128), held(4, 160, 128),
            held(8, 2, 32, 128), held(16, 32, 128),
            held(2, 256, 256, kind=F32), held(4, 256, 128), held(4, 256, 128), held(4, 2, 32, 128), held(2, 32, 256),
            dma((6,)), dma((4,)), dma((4,)), dma((4,)), dma, dma, dma((2,)), dma((2,)),
            dma, dma, dma((4,)), dma((4,)), dma((4,)), dma((4,)), dma, dma,
            dma((4,)), dma((4,)), dma((4,)), dma((2,)), dma((2,)), dma((2,)),
        ],
        compiler_params=pltpu.CompilerParams(collective_id=0, has_side_effects=True, vmem_limit_bytes=VMEM_LIMIT),
        name="layer",
    )(item_owner.reshape(1, 128), item_row.reshape(1, 128), lengths, table, cotangent, w_uvqk, w_out)

    grad_table, grad_uvqk, grad_out = pl.pallas_call(
        finish_kernel,
        out_shape=(shape((256, 512), F32), shape((32, 64), F32), shape((8, 64), F32)),
        in_specs=[vmem] * 2,
        out_specs=(vmem,) * 3,
        name="finish",
    )(shared, sums)
    return grad_table, grad_uvqk.T, grad_out.T


def solution(mesh):
    in_specs = (
        P("wide", None),
        P(("wide", "narrow"), None),
        P(("wide", "narrow")),
        P(("wide", "narrow"), None),
        P(("wide", "narrow"), None),
        P(),
        P(),
    )
    out_specs = (P("wide", None), P("narrow", "wide"), P("narrow", "wide"))
    return jax.shard_map(on_device, mesh=mesh, in_specs=in_specs, out_specs=out_specs, check_vma=False)
```

```python
import jax
import jax.numpy as jnp
from jax import lax
from jax.experimental import pallas as pl
from jax.experimental.pallas import tpu as pltpu
from jax.sharding import PartitionSpec as P

HEADS = 8
EPS = 1e-05
MESH = pl.DeviceIdType.MESH
F32, BF16, I32 = jnp.float32, jnp.bfloat16, jnp.int32
VMEM_LIMIT = 63 * 1024 * 1024


def div(value, by):
    return lax.div(value, jnp.int32(by))


def rem(value, by):
    return lax.rem(value, jnp.int32(by))


def coordinates():
    wide, narrow = lax.axis_index("wide"), lax.axis_index("narrow")
    return div(wide, 16), rem(wide, 16), div(narrow, 2), rem(narrow, 2)


def shard_z(y, c, b):
    return 2 * (rem(y + 2 * b, 4) + 4 * c) + 1 - b


def holder_of(z):
    b = 1 - rem(z, 2)
    half = div(z, 2)
    y = rem(rem(half, 4) + 4 - 2 * b, 4)
    return 2 * y + div(half, 4), b


def member(step, x, y, c, a, b):
    far = (div(step, 16), rem(div(step, 4), 4))
    dx, dy = [jnp.where(i == 0, 2, jnp.where(i == 1, 1, jnp.where(i == 2, 3, 0))) for i in far]
    to_x, to_y = rem(x + dx, 4), rem(y + dy, 4)
    to_b, to_c = rem(b + 1 + rem(div(step, 2), 2), 2), rem(c + 1 + rem(step, 2), 2)
    return to_x * 16 + shard_z(to_y, to_c, to_b), (to_x * 16 + 2 * a + to_b, 2 * to_y + to_c)


def signal(sem, device):
    pl.semaphore_signal(sem, inc=1, device_id=device, device_id_type=MESH)


def send(src, dst, send_sem, recv_sem, device):
    pltpu.make_async_remote_copy(
        src_ref=src, dst_ref=dst, send_sem=send_sem, recv_sem=recv_sem, device_id=device, device_id_type=MESH
    ).start()


def waiter(ref, send_sem, recv_sem, device):
    return pltpu.make_async_remote_copy(
        src_ref=ref, dst_ref=ref, send_sem=send_sem, recv_sem=recv_sem, device_id=device, device_id_type=MESH
    )


def iota(shape, dim):
    return lax.broadcasted_iota(I32, shape, dim)


def onehot(hits):
    return jnp.where(hits, 1.0, 0.0).astype(BF16)


def dot(left, right, contract=((1,), (0,))):
    return lax.dot_general(left, right, (contract, ((), ())), preferred_element_type=F32)


def ranks(owner_t, owner_s):
    sub, lane = iota((128, 128), 0), iota((128, 128), 1)
    same = owner_t == owner_s
    across = jnp.sum(jnp.where(same & (sub < lane), 1.0, 0.0), axis=0, keepdims=True)
    down = jnp.sum(jnp.where(same & (lane < sub), 1.0, 0.0), axis=1, keepdims=True)
    return down, across


def to_blocks(first, second, lanes):
    return jnp.concatenate([first.reshape(64, 8, lanes), second.reshape(64, 8, lanes)], axis=1).astype(BF16)


def mean_rows(values):
    return jnp.mean(values, axis=-1, keepdims=True)


def norm_back(grad, normed, scale):
    return scale * (grad - mean_rows(grad) - normed * mean_rows(grad * normed))


def weights_of_pairs(lengths):
    sub, lane = iota((128, 128), 0), iota((128, 128), 1)
    seg_t, seg_s = jnp.zeros((128, 128), I32), jnp.zeros((128, 128), I32)
    total = jnp.zeros((1, 1), I32)
    for i in range(6):
        total = total + lengths[0:1, i : i + 1]
        seg_t = seg_t + jnp.where(sub >= total, 1, 0)
        seg_s = seg_s + jnp.where(lane >= total, 1, 0)
    own_length = jnp.ones((128, 128), F32)
    for i in range(6):
        own_length = jnp.where(seg_t == i, lengths[0:1, i : i + 1].astype(F32), own_length)
    return jnp.where((seg_t == seg_s) & (lane <= sub), 1.0 / own_length, 0.0)


def layer_kernel(
    owner_hbm, row_hbm, lengths_hbm, table, cotangent_hbm, w_uvqk_hbm, w_out_hbm, shared, out_w,
    owner, row, lengths, cotangent, w_uvqk, w_out, own_shard, shard, ask_out, asked, chosen, reply_out, replies,
    pre, act, grad_act, grad_pre, grads, rows_out, rows_in, pair_in, x_out, y_out, x_in, y_in, x_mid, y_mid, xy_in, yx_in,
    line_out, line_in, sums, chain_in, chain_out, piece_in, share,
    load_sem, shard_send, shard_recv, pass_send, ask_send, ask_recv, reply_send, reply_recv,
    rows_send, rows_recv, pair_send, pair_recv, plane_send, plane_recv, line_send, line_recv,
    chain_send, chain_recv, piece_recv, share_send, share_recv, keep_sem,
):
    x, z, y, c = coordinates()
    wide = x * 16 + z
    a, b = div(z, 2), rem(z, 2)
    narrow = 2 * y + c
    here = (wide, narrow)
    my_z = shard_z(y, c, b)
    me = x * 16 + my_z
    to_narrow, to_b = holder_of(z)
    is_source = to_narrow == narrow
    away = rem(z - my_z + 16, 16)
    outward = jnp.where(away < 8, 1, -1)
    hops = jnp.where(away < 8, away, 16 - away)
    is_relay = hops == 3
    is_far = hops > 3
    upper = div(z, 8)
    in_half = (upper == c).astype(I32)
    barrier = pltpu.get_barrier_semaphore()

    def on_line(at_z):
        return x * 16 + rem(at_z + 32, 16), narrow

    loads = []
    for i, (src, dst) in enumerate(
        [(owner_hbm, owner), (row_hbm, row), (lengths_hbm, lengths), (w_uvqk_hbm, w_uvqk), (cotangent_hbm, cotangent), (w_out_hbm, w_out)]
        + [(table.at[:, pl.ds(128 * piece, 128)], own_shard.at[piece]) for piece in range(4)]
    ):
        loads.append(pltpu.make_async_copy(src, dst, load_sem.at[i]))
        loads[-1].start()

    parent = jnp.where(hops > 3, my_z + 3 * outward, my_z)
    signal(barrier, on_line(parent))

    def greet(step, carry):
        signal(barrier, member(step, x, y, c, a, b)[1])
        return carry

    lax.fori_loop(0, 63, greet, 0)

    loads[0].wait()
    loads[1].wait()
    owner_s = jnp.broadcast_to(owner[...].astype(F32), (128, 128))
    owner_t = owner_s.T
    rank_t, rank_s = ranks(owner_t, owner_s)
    slot_s = (owner_s * 8.0 + rank_s)[0:1].astype(I32)
    slot_t = (owner_t * 16.0 + rank_t)[:, 0:1].astype(I32)
    slots = onehot(iota((512, 128), 0) == slot_s)
    named = (jnp.broadcast_to(row[...].astype(F32), (128, 128)).T + 1.0).astype(BF16)
    ask_out[...] = dot(slots, named).reshape(64, 8, 128)

    for piece in range(4):
        loads[6 + piece].wait()
    pl.semaphore_wait(barrier, 63 + 4 * is_source.astype(I32) + 2 * is_relay.astype(I32))

    @pl.when(is_source)
    def _():
        for piece in range(4):
            for step in (3, -3, 1, -1):
                send(
                    own_shard.at[piece], shard.at[piece],
                    shard_send.at[piece], shard_recv.at[piece], on_line(z + step),
                )

    def ask(step, carry):
        rank, device = member(step, x, y, c, a, b)
        send(ask_out.at[rank], asked.at[me], ask_send, ask_recv, device)
        return carry

    lax.fori_loop(0, 63, ask, 0)
    asked[pl.ds(me, 1)] = ask_out[pl.ds(me, 1)]
    most = pl.ds(0, 63)

    @pl.when(is_relay)
    def _():
        for piece in range(4):
            waiter(shard.at[piece], shard_send.at[piece], shard_recv.at[piece], here).wait_recv()
            for step in (4, 2):
                send(
                    shard.at[piece], shard.at[piece],
                    pass_send.at[piece], shard_recv.at[piece], on_line(z + outward * step),
                )

    waiter(asked.at[most], ask_send, ask_recv, here).wait_recv()
    wanted = asked[...].reshape(512, 128).astype(I32)
    wanted = jnp.concatenate([wanted, wanted], axis=1)
    chosen[...] = onehot(wanted == iota((512, 256), 1) + 1)
    for half in range(2):
        @pl.when(jnp.logical_not(is_relay))
        def _(half=half):
            for piece in (2 * half, 2 * half + 1):
                waiter(shard.at[piece], shard_send.at[piece], shard_recv.at[piece], here).wait_recv()

        picked = dot(chosen[...], jnp.concatenate([shard[2 * half], shard[2 * half + 1]], axis=1))
        reply_out[half] = to_blocks(picked[:, 0:128], picked[:, 128:256], 128)

        def answer(step, carry, half=half):
            rank, device = member(step, x, y, c, a, b)
            send(
                reply_out.at[half, rank], replies.at[half, me],
                reply_send.at[half], reply_recv.at[half], device,
            )
            return carry

        lax.fori_loop(0, 63, answer, 0)
        replies[half, pl.ds(me, 1)] = reply_out[half, pl.ds(me, 1)]

    loads[2].wait()
    weight = weights_of_pairs(lengths)
    spots = iota((128, 1024), 1)
    finds = (onehot(spots == slot_t), onehot(spots == slot_t + 8))
    parts = []
    for half in range(2):
        waiter(replies.at[half, most], reply_send.at[half], reply_recv.at[half], here).wait_recv()
        arrived = replies[half].reshape(1024, 128)
        parts += [dot(finds[0], arrived), dot(finds[1], arrived)]
    embedded = jnp.concatenate(parts, axis=1)
    center = embedded - mean_rows(embedded)
    embed_scale = lax.rsqrt(mean_rows(center * center) + EPS)
    embed_norm = center * embed_scale
    normed = embed_norm.astype(BF16)

    loads[3].wait()
    for part in range(4):
        cols = pl.ds(512 * part, 512)
        value = dot(normed, w_uvqk[:, cols])
        pre[:, cols] = value
        act[:, cols] = (value * jax.nn.sigmoid(value)).astype(BF16)

    first_half = iota((128, 128), 1) < 64
    keep = (first_half, jnp.logical_not(first_half))
    zero = jnp.zeros((128, 128), BF16)
    mixed = []
    for pair in range(4):
        q = act[:, 1024 + 128 * pair : 1152 + 128 * pair]
        k = act[:, 1536 + 128 * pair : 1664 + 128 * pair]
        v = act[:, 512 + 128 * pair : 640 + 128 * pair]
        both = jnp.zeros((128, 128), F32)
        for head in range(2):
            score = dot(jnp.where(keep[head], q, zero), k, ((1,), (1,))) * 0.125
            attention = (score * jax.nn.sigmoid(score) * weight).astype(BF16)
            both = both + dot(attention, jnp.where(keep[head], v, zero))
        mixed.append(both)
    mixture = jnp.concatenate(mixed, axis=1)
    center = mixture - mean_rows(mixture)
    mix_scale = lax.rsqrt(mean_rows(center * center) + EPS)
    mix_norm = center * mix_scale
    gate = act[:, 0:512].astype(F32)
    gated = (mix_norm * gate).astype(BF16)

    loads[4].wait()
    loads[5].wait()
    cot = cotangent[...]

    def back(part, grad_normed):
        cols = pl.ds(512 * part, 512)
        value = pre[:, cols]
        gain = jax.nn.sigmoid(value)
        grad_pre[:, cols] = (grad_act[:, cols] * (gain * (1.0 + value * (1.0 - gain)))).astype(BF16)
        return grad_normed + dot(grad_pre[:, cols], w_uvqk[:, cols], ((1,), (1,)))

    grad_gated = dot(cot, w_out[...], ((1,), (1,)))
    grad_act[:, 0:512] = grad_gated * mix_norm
    grad_normed = back(0, jnp.zeros((128, 512), F32))
    grad_mix = norm_back(grad_gated * gate, mix_norm, mix_scale).astype(BF16)
    for pair in range(4):
        q = act[:, 1024 + 128 * pair : 1152 + 128 * pair]
        k = act[:, 1536 + 128 * pair : 1664 + 128 * pair]
        v = act[:, 512 + 128 * pair : 640 + 128 * pair]
        g = grad_mix[:, 128 * pair : 128 * pair + 128]
        grad_q, grad_k, grad_v = [jnp.zeros((128, 128), F32)] * 3
        for head in range(2):
            q_one, k_one, v_one, g_one = [jnp.where(keep[head], part, zero) for part in (q, k, v, g)]
            score = dot(q_one, k, ((1,), (1,))) * 0.125
            gain = jax.nn.sigmoid(score)
            attention = (score * gain * weight).astype(BF16)
            grad_att = dot(g_one, v, ((1,), (1,)))
            grad_score = (grad_att * weight * (gain * (1.0 + score * (1.0 - gain))) * 0.125).astype(BF16)
            grad_v = grad_v + dot(attention, g_one, ((0,), (0,)))
            grad_q = grad_q + dot(grad_score, k_one)
            grad_k = grad_k + dot(grad_score, q_one, ((0,), (0,)))
        grad_act[:, 512 + 128 * pair : 640 + 128 * pair] = grad_v
        grad_act[:, 1024 + 128 * pair : 1152 + 128 * pair] = grad_q
        grad_act[:, 1536 + 128 * pair : 1664 + 128 * pair] = grad_k
    for part in range(1, 4):
        grad_normed = back(part, grad_normed)
    grad_embed = (cot.astype(F32) + norm_back(grad_normed, embed_norm, embed_scale)).astype(BF16)

    given = dot(slots, grad_embed)
    rows_out[...] = to_blocks(given[:, 0:256], given[:, 256:512], 256)

    def give_rows(step, carry):
        rank, device = member(step, x, y, c, a, b)
        send(rows_out.at[rank], rows_in.at[me], rows_send, rows_recv, device)
        return carry

    lax.fori_loop(0, 63, give_rows, 0)
    rows_in[pl.ds(me, 1)] = rows_out[pl.ds(me, 1)]

    grad_o = dot(cot, gated, ((0,), (0,))).astype(BF16)
    partner = (wide, 2 * y + 1 - c)
    for part in range(4):
        grad_u = dot(grad_pre[:, pl.ds(512 * part, 512)], normed, ((0,), (0,))).astype(BF16)
        for side in range(2):
            grads[part, side, 0:256] = grad_u[256 * side : 256 * side + 256]
            grads[part, side, 256:320] = grad_o[128 * part + 64 * side : 128 * part + 64 * side + 64]
        send(grads.at[part, 1 - c], pair_in.at[part], pair_send.at[part], pair_recv.at[part], partner)
    for part in range(4):
        waiter(pair_in.at[part], pair_send.at[part], pair_recv.at[part], here).wait()
        mine = grads[part, pl.ds(c, 1)].reshape(320, 512).astype(F32)
        both = (mine + pair_in[part].astype(F32)).astype(BF16)
        x_out[part] = both[0:160]
        for to in range(4):
            y_out[to, part] = both[160:320, 128 * to : 128 * to + 128]
    for step in range(1, 4):
        to_x, to_y = rem(x + step, 4), rem(y + step, 4)
        send(
            x_out.at[to_x], x_in.at[x], plane_send.at[0], plane_recv.at[0],
            (to_x * 16 + z, narrow),
        )
        send(
            y_out.at[to_y], y_in.at[y],
            plane_send.at[1], plane_recv.at[1], (wide, 2 * to_y + c),
        )
    x_in[pl.ds(x, 1)] = x_out[pl.ds(x, 1)]
    y_in[pl.ds(y, 1)] = y_out[pl.ds(y, 1)]

    waiter(rows_in.at[most], rows_send, rows_recv, here).wait()
    arrived = rows_in[...].astype(F32)
    for half in range(2):
        sums[half] = dot(chosen[...], arrived[:, 8 * half : 8 * half + 8].reshape(512, 256).astype(BF16), ((0,), (0,)))

    child = (hops == 7).astype(I32)
    place = jnp.where(hops == 1, 0, 1) + 1 - outward

    def give_pieces(piece, values):
        chain_out[piece] = values.astype(BF16)

        def give(step, carry):
            to = rem(narrow + step, 8)
            send(
                chain_out.at[piece, pl.ds(pl.multiple_of(32 * to, 32), 32)], piece_in.at[piece, place],
                chain_send.at[piece], piece_recv.at[piece], (x * 16 + my_z, to),
            )
            return carry

        lax.fori_loop(0, 8, give, 0)

    def own_sums(piece):
        return sums[piece // 2, :, 128 * (piece % 2) : 128 * (piece % 2) + 128]

    @pl.when(is_far)
    def _():
        for piece in range(4):
            chain_out[piece] = own_sums(piece).astype(BF16)
            send(
                chain_out.at[piece], chain_in.at[piece, child],
                chain_send.at[piece], chain_recv.at[piece], on_line(parent),
            )

    @pl.when(hops == 1)
    def _():
        for piece in range(4):
            give_pieces(piece, own_sums(piece))

    three = pl.ds(0, 3)

    def add_up(ref):
        total = ref[0].astype(F32)
        for step in range(1, ref.shape[0]):
            total = total + ref[step].astype(F32)
        return total

    waiter(x_in.at[three], plane_send.at[0], plane_recv.at[0], here).wait()
    total = add_up(x_in).astype(BF16)
    for to in range(4):
        x_mid[to] = total[:, 128 * to : 128 * to + 128]
    for step in range(1, 4):
        to_y = rem(y + step, 4)
        send(
            x_mid.at[to_y], xy_in.at[y],
            plane_send.at[2], plane_recv.at[2], (wide, 2 * to_y + c),
        )
    xy_in[pl.ds(y, 1)] = x_mid[pl.ds(y, 1)]
    waiter(y_in.at[three], plane_send.at[1], plane_recv.at[1], here).wait()
    y_mid[...] = add_up(y_in).astype(BF16)
    for step in range(1, 4):
        to_x = rem(x + step, 4)
        send(y_mid.at[to_x], yx_in.at[x], plane_send.at[3], plane_recv.at[3], (to_x * 16 + z, narrow))
    yx_in[pl.ds(x, 1)] = y_mid[pl.ds(x, 1)]
    @pl.when(is_relay)
    def _():
        for piece in range(4):
            waiter(chain_in.at[piece], chain_send.at[piece], chain_recv.at[piece], here).wait_recv()
            give_pieces(piece, own_sums(piece) + add_up(chain_in.at[piece]))

    waiter(xy_in.at[three], plane_send.at[2], plane_recv.at[2], here).wait()
    waiter(yx_in.at[three], plane_send.at[3], plane_recv.at[3], here).wait()
    total = jnp.concatenate([add_up(xy_in), add_up(yx_in)], axis=0)
    rolled = pltpu.roll(total, 64, 1)
    left = iota((16, 128), 1) < 64
    for step in range(8):
        top, bottom = slice(32 * step, 32 * step + 16), slice(32 * step + 16, 32 * step + 32)
        rest = slice(256 + 8 * step, 264 + 8 * step)
        first = jnp.where(left, total[top], rolled[bottom])
        second = jnp.where(left, rolled[top], total[bottom])
        for core, packed, values in ((0, first, total), (1, second, rolled)):
            line_out[step, core] = jnp.concatenate([packed, values[rest], jnp.zeros((8, 128), F32)], axis=0).astype(BF16)

    def give_line(step, carry):
        to_z = 8 * c + step
        for core in range(2):
            own = jnp.logical_and(to_z == z, c == core)

            @pl.when(jnp.logical_not(own))
            def _():
                send(line_out.at[step, core], line_in.at[z], line_send, line_recv, (x * 16 + to_z, 2 * y + core))

            @pl.when(own)
            def _():
                line_in[pl.ds(z, 1)] = line_out[pl.ds(step, 1), core]

        return carry

    lax.fori_loop(0, 8, give_line, 0)

    keeps = []
    for half in range(2):
        quarters = []
        for piece in (2 * half, 2 * half + 1):
            waiter(piece_in.at[piece], chain_send.at[piece], piece_recv.at[piece], here).wait_recv()
            quarters.append(add_up(piece_in.at[piece]))
        share[half] = jnp.concatenate(quarters, axis=1).astype(BF16)
        keeps.append(pltpu.make_async_copy(share.at[half], shared.at[half, narrow], keep_sem.at[half]))
        keeps[-1].start()

        def give_share(step, carry, half=half):
            send(
                share.at[half], shared.at[half, narrow],
                share_send.at[half], share_recv.at[half], (wide, rem(narrow + step, 8)),
            )
            return carry

        lax.fori_loop(1, 8, give_share, 0)

    @pl.when(in_half == 1)
    def _():
        waiter(line_in.at[pl.ds(0, 15)], line_send, line_recv, here).wait()

    @pl.when(in_half == 0)
    def _():
        waiter(line_in, line_send, line_recv, here).wait()

    total = add_up(line_in)
    out_w[0:16] = total[0:16, 0:64]
    out_w[16:32] = total[0:16, 64:128]
    out_w[32:40] = total[16:24, 0:64]

    waiter(asked.at[most], ask_send, ask_recv, here).wait_send()
    for half in range(2):
        waiter(replies.at[half, most], reply_send.at[half], reply_recv.at[half], here).wait_send()

    for piece in range(4):

        @pl.when(is_source)
        def _(piece=piece):
            for step in range(4):
                waiter(shard.at[piece], shard_send.at[piece], shard_recv.at[piece], here).wait_send()

        @pl.when(is_relay)
        def _(piece=piece):
            for step in range(2):
                waiter(shard.at[piece], pass_send.at[piece], shard_recv.at[piece], here).wait_send()

        waiter(chain_out.at[piece], chain_send.at[piece], chain_recv.at[piece], here).wait_send()

    for half in range(2):
        waiter(shared.at[half, pl.ds(0, 7)], share_send.at[half], share_recv.at[half], here).wait()
        keeps[half].wait()


def finish_kernel(shared, sums, out_table, out_u, out_o):
    for half in range(2):
        out_table[:, 256 * half : 256 * half + 256] = shared[half].reshape(256, 256).astype(F32)
    out_u[...] = sums[0:32]
    out_o[...] = sums[32:40]


def on_device(table, item_owner, item_row, lengths, cotangent, w_uvqk, w_out):
    vmem = pl.BlockSpec(memory_space=pltpu.VMEM)
    anywhere = pl.BlockSpec(memory_space=pl.ANY)
    dma = pltpu.SemaphoreType.DMA
    shape = jax.ShapeDtypeStruct

    def held(*sizes, kind=BF16):
        return pltpu.VMEM(sizes, kind)

    shared, sums = pl.pallas_call(
        layer_kernel,
        out_shape=(shape((2, 8, 32, 256), BF16), shape((40, 64), F32)),
        in_specs=[anywhere] * 7,
        out_specs=(anywhere, vmem),
        scratch_shapes=[
            held(1, 128, kind=I32), held(1, 128, kind=I32), held(1, 6, kind=I32),
            held(128, 512), held(512, 2048), held(512, 512),
            held(4, 256, 128), held(4, 256, 128), held(64, 8, 128, kind=F32), held(64, 8, 128, kind=F32), held(512, 256),
            held(2, 64, 16, 128), held(2, 64, 16, 128),
            held(128, 2048, kind=F32), held(128, 2048), held(128, 2048, kind=F32), held(128, 2048),
            held(4, 2, 320, 512), held(64, 16, 256), held(64, 16, 256),
            held(4, 320, 512), held(4, 160, 512), held(4, 4, 160, 128),
            held(4, 160, 512), held(4, 4, 160, 128), held(4, 160, 128), held(4, 160, 128),
            held(4, 160, 128), held(4, 160, 128),
            held(8, 2, 32, 128), held(16, 32, 128),
            held(2, 256, 256, kind=F32), held(4, 2, 256, 128), held(4, 256, 128), held(4, 4, 32, 128), held(2, 32, 256),
            dma((10,)), dma((4,)), dma((4,)), dma((4,)), dma, dma, dma((2,)), dma((2,)),
            dma, dma, dma((4,)), dma((4,)), dma((4,)), dma((4,)), dma, dma,
            dma((4,)), dma((4,)), dma((4,)), dma((2,)), dma((2,)), dma((2,)),
        ],
        compiler_params=pltpu.CompilerParams(collective_id=0, has_side_effects=True, vmem_limit_bytes=VMEM_LIMIT),
        name="layer",
    )(item_owner.reshape(1, 128), item_row.reshape(1, 128), lengths, table, cotangent, w_uvqk, w_out)

    grad_table, grad_uvqk, grad_out = pl.pallas_call(
        finish_kernel,
        out_shape=(shape((256, 512), F32), shape((32, 64), F32), shape((8, 64), F32)),
        in_specs=[vmem] * 2,
        out_specs=(vmem,) * 3,
        name="finish",
    )(shared, sums)
    return grad_table, grad_uvqk.T, grad_out.T


def solution(mesh):
    in_specs = (
        P("wide", None),
        P(("wide", "narrow"), None),
        P(("wide", "narrow")),
        P(("wide", "narrow"), None),
        P(("wide", "narrow"), None),
        P(),
        P(),
    )
    out_specs = (P("wide", None), P("narrow", "wide"), P("narrow", "wide"))
    return jax.shard_map(on_device, mesh=mesh, in_specs=in_specs, out_specs=out_specs, check_vma=False)
```

```python
import jax
import jax.numpy as jnp
from jax import lax
from jax.experimental import pallas as pl
from jax.experimental.pallas import tpu as pltpu
from jax.sharding import PartitionSpec as P

HEADS = 8
EPS = 1e-05
MESH = pl.DeviceIdType.MESH
F32, BF16, I32 = jnp.float32, jnp.bfloat16, jnp.int32
VMEM_LIMIT = 63 * 1024 * 1024


def div(value, by):
    return lax.div(value, jnp.int32(by))


def rem(value, by):
    return lax.rem(value, jnp.int32(by))


def coordinates():
    wide, narrow = lax.axis_index("wide"), lax.axis_index("narrow")
    return div(wide, 16), rem(wide, 16), div(narrow, 2), rem(narrow, 2)


def shard_z(y, c, b):
    return 2 * (rem(y + 2 * b, 4) + 4 * c) + 1 - b


def holder_of(z):
    b = 1 - rem(z, 2)
    half = div(z, 2)
    y = rem(rem(half, 4) + 4 - 2 * b, 4)
    return 2 * y + div(half, 4), b


def member(step, x, y, c, a, b):
    far = (div(step, 16), rem(div(step, 4), 4))
    dx, dy = [jnp.where(i == 0, 2, jnp.where(i == 1, 1, jnp.where(i == 2, 3, 0))) for i in far]
    to_x, to_y = rem(x + dx, 4), rem(y + dy, 4)
    to_b, to_c = rem(b + 1 + rem(div(step, 2), 2), 2), rem(c + 1 + rem(step, 2), 2)
    return to_x * 16 + shard_z(to_y, to_c, to_b), (to_x * 16 + 2 * a + to_b, 2 * to_y + to_c)


def signal(sem, device):
    pl.semaphore_signal(sem, inc=1, device_id=device, device_id_type=MESH)


def send(src, dst, send_sem, recv_sem, device):
    pltpu.make_async_remote_copy(
        src_ref=src, dst_ref=dst, send_sem=send_sem, recv_sem=recv_sem, device_id=device, device_id_type=MESH
    ).start()


def waiter(ref, send_sem, recv_sem, device):
    return pltpu.make_async_remote_copy(
        src_ref=ref, dst_ref=ref, send_sem=send_sem, recv_sem=recv_sem, device_id=device, device_id_type=MESH
    )


def iota(shape, dim):
    return lax.broadcasted_iota(I32, shape, dim)


def onehot(hits):
    return jnp.where(hits, 1.0, 0.0).astype(BF16)


def dot(left, right, contract=((1,), (0,))):
    return lax.dot_general(left, right, (contract, ((), ())), preferred_element_type=F32)


def ranks(owner_t, owner_s):
    sub, lane = iota((128, 128), 0), iota((128, 128), 1)
    same = owner_t == owner_s
    across = jnp.sum(jnp.where(same & (sub < lane), 1.0, 0.0), axis=0, keepdims=True)
    down = jnp.sum(jnp.where(same & (lane < sub), 1.0, 0.0), axis=1, keepdims=True)
    return down, across


def to_blocks(first, second, lanes):
    return jnp.concatenate([first.reshape(64, 8, lanes), second.reshape(64, 8, lanes)], axis=1).astype(BF16)


def mean_rows(values):
    return jnp.mean(values, axis=-1, keepdims=True)


def norm_back(grad, normed, scale):
    return scale * (grad - mean_rows(grad) - normed * mean_rows(grad * normed))


def weights_of_pairs(lengths):
    sub, lane = iota((128, 128), 0), iota((128, 128), 1)
    seg_t, seg_s = jnp.zeros((128, 128), I32), jnp.zeros((128, 128), I32)
    total = jnp.zeros((1, 1), I32)
    for i in range(6):
        total = total + lengths[0:1, i : i + 1]
        seg_t = seg_t + jnp.where(sub >= total, 1, 0)
        seg_s = seg_s + jnp.where(lane >= total, 1, 0)
    own_length = jnp.ones((128, 128), F32)
    for i in range(6):
        own_length = jnp.where(seg_t == i, lengths[0:1, i : i + 1].astype(F32), own_length)
    return jnp.where((seg_t == seg_s) & (lane <= sub), 1.0 / own_length, 0.0)


def layer_kernel(
    owner_hbm, row_hbm, lengths_hbm, table, cotangent_hbm, w_uvqk_hbm, w_out_hbm, shared, out_w,
    owner, row, lengths, cotangent, w_uvqk, w_out, own_shard, shard, ask_out, asked, chosen, gathers, reply_out, replies,
    slope, act, held_att, att_slope, grad_act, grad_pre, grads, rows_out, rows_in, pair_in, x_out, y_out, x_in, y_in, x_mid, y_mid, xy_in, yx_in,
    line_out, line_in, sums, chain_in, chain_out, piece_in, share, held_w,
    load_sem, shard_send, shard_recv, pass_send, ask_send, ask_recv, reply_send, reply_recv,
    rows_send, rows_recv, pair_send, pair_recv, plane_send, plane_recv, line_send, line_recv,
    chain_send, chain_recv, piece_recv, share_send, share_recv, keep_sem,
):
    x, z, y, c = coordinates()
    wide = x * 16 + z
    a, b = div(z, 2), rem(z, 2)
    narrow = 2 * y + c
    here = (wide, narrow)
    my_z = shard_z(y, c, b)
    me = x * 16 + my_z
    to_narrow, to_b = holder_of(z)
    is_source = to_narrow == narrow
    away = rem(z - my_z + 16, 16)
    outward = jnp.where(away < 8, 1, -1)
    hops = jnp.where(away < 8, away, 16 - away)
    is_relay = hops == 3
    passes_on = jnp.logical_or(hops == 3, hops == 5)
    is_far = hops > 3
    upper = div(z, 8)
    in_half = (upper == c).astype(I32)
    barrier = pltpu.get_barrier_semaphore()

    def on_line(at_z):
        return x * 16 + rem(at_z + 32, 16), narrow

    loads = []
    for i, (src, dst) in enumerate(
        [(owner_hbm, owner), (row_hbm, row), (lengths_hbm, lengths), (w_uvqk_hbm, w_uvqk), (cotangent_hbm, cotangent), (w_out_hbm, w_out)]
        + [(table.at[:, pl.ds(128 * piece, 128)], own_shard.at[piece]) for piece in range(4)]
    ):
        loads.append(pltpu.make_async_copy(src, dst, load_sem.at[i]))
        loads[-1].start()

    parent = jnp.where(hops > 3, my_z + 3 * outward, my_z)
    signal(barrier, on_line(jnp.where(hops > 3, z - 2 * outward, my_z)))

    def greet(step, carry):
        signal(barrier, member(step, x, y, c, a, b)[1])
        return carry

    lax.fori_loop(0, 63, greet, 0, unroll=7)

    loads[0].wait()
    loads[1].wait()
    owner_s = jnp.broadcast_to(owner[...].astype(F32), (128, 128))
    owner_t = owner_s.T
    rank_t, rank_s = ranks(owner_t, owner_s)
    slot_s = (owner_s * 8.0 + rank_s)[0:1].astype(I32)
    slot_t = (owner_t * 16.0 + rank_t)[:, 0:1].astype(I32)
    slots = onehot(iota((512, 128), 0) == slot_s)
    named = (jnp.broadcast_to(row[...].astype(F32), (128, 128)).T + 1.0).astype(BF16)
    ask_out[...] = dot(slots, named).reshape(64, 8, 128)

    for piece in range(4):
        loads[6 + piece].wait()
    pl.semaphore_wait(barrier, 63 + 4 * is_source.astype(I32) + passes_on.astype(I32))

    @pl.when(is_source)
    def _():
        for steps in ((3, -3), (1, -1)):
            for piece in range(4):
                for step in steps:
                    send(
                        own_shard.at[piece], shard.at[piece],
                        shard_send.at[piece], shard_recv.at[piece], on_line(z + step),
                    )

    def ask(step, carry):
        rank, device = member(step, x, y, c, a, b)
        send(ask_out.at[rank], asked.at[me], ask_send, ask_recv, device)
        return carry

    lax.fori_loop(0, 63, ask, 0, unroll=7)
    asked[pl.ds(me, 1)] = ask_out[pl.ds(me, 1)]
    most = pl.ds(0, 63)

    @pl.when(passes_on)
    def _():
        for piece in range(4):
            waiter(shard.at[piece], shard_send.at[piece], shard_recv.at[piece], here).wait_recv()
            send(
                shard.at[piece], shard.at[piece],
                pass_send.at[piece], shard_recv.at[piece], on_line(z + outward * 2),
            )

    waiter(asked.at[most], ask_send, ask_recv, here).wait_recv()
    wanted = asked[...].reshape(512, 128).astype(I32)
    wanted = jnp.concatenate([wanted, wanted], axis=1)
    chosen[...] = onehot(wanted == iota((512, 256), 1) + 1)
    @pl.when(jnp.logical_not(passes_on))
    def _():
        for piece in range(4):
            waiter(shard.at[piece], shard_send.at[piece], shard_recv.at[piece], here).wait_recv()

    first = dot(chosen[...], jnp.concatenate([shard[0], shard[1]], axis=1))
    second = dot(chosen[...], jnp.concatenate([shard[2], shard[3]], axis=1))
    reply_out[...] = to_blocks(first, second, 256)

    def answer(step, carry):
        rank, device = member(step, x, y, c, a, b)
        send(reply_out.at[rank], replies.at[me], reply_send, reply_recv, device)
        return carry

    lax.fori_loop(0, 63, answer, 0)
    replies[pl.ds(me, 1)] = reply_out[pl.ds(me, 1)]

    none = jnp.zeros((64, 8, 256), F32)
    hits = chosen[...].astype(F32).reshape(64, 8, 256)
    for half in range(2):
        spread = jnp.concatenate([none, hits] if half else [hits, none], axis=1)
        gathers[256 * half : 256 * half + 256] = spread.reshape(1024, 256).T.astype(BF16)
    loads[2].wait()
    weight = weights_of_pairs(lengths)
    spots = iota((128, 1024), 1)
    finds = (onehot(spots == slot_t), onehot(spots == slot_t + 8))
    waiter(replies.at[most], reply_send, reply_recv, here).wait_recv()
    arrived = replies[...].reshape(1024, 256)
    embedded = jnp.concatenate([dot(finds[0], arrived), dot(finds[1], arrived)], axis=1)
    center = embedded - mean_rows(embedded)
    embed_scale = lax.rsqrt(mean_rows(center * center) + EPS)
    embed_norm = center * embed_scale
    normed = embed_norm.astype(BF16)

    loads[3].wait()
    for part in range(4):
        cols = pl.ds(512 * part, 512)
        value = dot(normed, w_uvqk[:, cols])
        gain = jax.nn.sigmoid(value)
        act[:, cols] = (value * gain).astype(BF16)
        slope[:, cols] = gain * (1.0 + value * (1.0 - gain))

    first_half = iota((128, 128), 1) < 64
    keep = (first_half, jnp.logical_not(first_half))
    zero = jnp.zeros((128, 128), BF16)
    mixed = []
    for pair in range(4):
        q = act[:, 1024 + 128 * pair : 1152 + 128 * pair]
        k = act[:, 1536 + 128 * pair : 1664 + 128 * pair]
        v = act[:, 512 + 128 * pair : 640 + 128 * pair]
        both = jnp.zeros((128, 128), F32)
        for head in range(2):
            score = dot(jnp.where(keep[head], q, zero), k, ((1,), (1,))) * 0.125
            gain = jax.nn.sigmoid(score)
            attention = (score * gain * weight).astype(BF16)
            held_att[2 * pair + head] = attention
            att_slope[2 * pair + head] = weight * (gain * (1.0 + score * (1.0 - gain))) * 0.125
            both = both + dot(attention, jnp.where(keep[head], v, zero))
        mixed.append(both)
    mixture = jnp.concatenate(mixed, axis=1)
    center = mixture - mean_rows(mixture)
    mix_scale = lax.rsqrt(mean_rows(center * center) + EPS)
    mix_norm = center * mix_scale
    gate = act[:, 0:512].astype(F32)
    gated = (mix_norm * gate).astype(BF16)

    loads[4].wait()
    loads[5].wait()
    cot = cotangent[...]

    def back(part, grad_normed):
        cols = pl.ds(512 * part, 512)
        grad_pre[:, cols] = (grad_act[:, cols] * slope[:, cols]).astype(BF16)
        return grad_normed + dot(grad_pre[:, cols], w_uvqk[:, cols], ((1,), (1,)))

    grad_gated = dot(cot, w_out[...], ((1,), (1,)))
    grad_act[:, 0:512] = grad_gated * mix_norm
    grad_normed = back(0, jnp.zeros((128, 512), F32))
    grad_mix = norm_back(grad_gated * gate, mix_norm, mix_scale).astype(BF16)
    for pair in range(4):
        q = act[:, 1024 + 128 * pair : 1152 + 128 * pair]
        k = act[:, 1536 + 128 * pair : 1664 + 128 * pair]
        v = act[:, 512 + 128 * pair : 640 + 128 * pair]
        g = grad_mix[:, 128 * pair : 128 * pair + 128]
        grad_q, grad_k, grad_v = [jnp.zeros((128, 128), F32)] * 3
        for head in range(2):
            q_one, k_one, v_one, g_one = [jnp.where(keep[head], part, zero) for part in (q, k, v, g)]
            grad_att = dot(g_one, v, ((1,), (1,)))
            grad_score = (grad_att * att_slope[2 * pair + head]).astype(BF16)
            grad_v = grad_v + dot(held_att[2 * pair + head], g_one, ((0,), (0,)))
            grad_q = grad_q + dot(grad_score, k_one)
            grad_k = grad_k + dot(grad_score, q_one, ((0,), (0,)))
        grad_act[:, 512 + 128 * pair : 640 + 128 * pair] = grad_v
        grad_act[:, 1024 + 128 * pair : 1152 + 128 * pair] = grad_q
        grad_act[:, 1536 + 128 * pair : 1664 + 128 * pair] = grad_k
    for part in range(1, 4):
        grad_normed = back(part, grad_normed)
    grad_embed = (cot.astype(F32) + norm_back(grad_normed, embed_norm, embed_scale)).astype(BF16)

    given = dot(slots, grad_embed)
    rows_out[...] = to_blocks(given[:, 0:256], given[:, 256:512], 256)

    def give_rows(step, carry):
        rank, device = member(step, x, y, c, a, b)
        send(rows_out.at[rank], rows_in.at[me], rows_send, rows_recv, device)
        return carry

    lax.fori_loop(0, 63, give_rows, 0, unroll=7)
    rows_in[pl.ds(me, 1)] = rows_out[pl.ds(me, 1)]

    grad_o = dot(cot, gated, ((0,), (0,))).astype(BF16)
    partner = (wide, 2 * y + 1 - c)
    for part in range(4):
        grad_u = dot(grad_pre[:, pl.ds(512 * part, 512)], normed, ((0,), (0,))).astype(BF16)
        for side in range(2):
            grads[part, side, 0:256] = grad_u[256 * side : 256 * side + 256]
            grads[part, side, 256:320] = grad_o[128 * part + 64 * side : 128 * part + 64 * side + 64]
        send(grads.at[part, 1 - c], pair_in.at[part], pair_send.at[part], pair_recv.at[part], partner)
    for part in range(4):
        waiter(pair_in.at[part], pair_send.at[part], pair_recv.at[part], here).wait()
        mine = grads[part, pl.ds(c, 1)].reshape(320, 512).astype(F32)
        both = (mine + pair_in[part].astype(F32)).astype(BF16)
        x_out[part] = both[0:160]
        for to in range(4):
            y_out[to, part] = both[160:320, 128 * to : 128 * to + 128]
    for step in range(1, 4):
        to_x, to_y = rem(x + step, 4), rem(y + step, 4)
        send(
            x_out.at[to_x], x_in.at[x], plane_send.at[0], plane_recv.at[0],
            (to_x * 16 + z, narrow),
        )
        send(
            y_out.at[to_y], y_in.at[y],
            plane_send.at[1], plane_recv.at[1], (wide, 2 * to_y + c),
        )
    x_in[pl.ds(x, 1)] = x_out[pl.ds(x, 1)]
    y_in[pl.ds(y, 1)] = y_out[pl.ds(y, 1)]

    waiter(rows_in.at[most], rows_send, rows_recv, here).wait()
    sums[...] = dot(gathers[...], rows_in[...].reshape(1024, 256)).reshape(2, 256, 256)

    child = (hops == 7).astype(I32)
    place = jnp.where(hops == 1, 0, 1) + 1 - outward

    def give_pieces(piece, values):
        chain_out[piece] = values.astype(BF16)

        def give(step, carry):
            to = rem(narrow + step, 8)
            send(
                chain_out.at[piece, pl.ds(pl.multiple_of(32 * to, 32), 32)], piece_in.at[piece, place],
                chain_send.at[piece], piece_recv.at[piece], (x * 16 + my_z, to),
            )
            return carry

        lax.fori_loop(0, 8, give, 0)

    def own_sums(piece):
        return sums[piece // 2, :, 128 * (piece % 2) : 128 * (piece % 2) + 128]

    @pl.when(is_far)
    def _():
        for piece in range(4):
            chain_out[piece] = own_sums(piece).astype(BF16)
            send(
                chain_out.at[piece], chain_in.at[piece, child],
                chain_send.at[piece], chain_recv.at[piece], on_line(parent),
            )

    @pl.when(hops == 1)
    def _():
        for piece in range(4):
            give_pieces(piece, own_sums(piece))

    three = pl.ds(0, 3)

    def add_up(ref):
        total = ref[0].astype(F32)
        for step in range(1, ref.shape[0]):
            total = total + ref[step].astype(F32)
        return total

    waiter(x_in.at[three], plane_send.at[0], plane_recv.at[0], here).wait()
    total = add_up(x_in).astype(BF16)
    for to in range(4):
        x_mid[to] = total[:, 128 * to : 128 * to + 128]
    for step in range(1, 4):
        to_y = rem(y + step, 4)
        send(
            x_mid.at[to_y], xy_in.at[y],
            plane_send.at[2], plane_recv.at[2], (wide, 2 * to_y + c),
        )
    xy_in[pl.ds(y, 1)] = x_mid[pl.ds(y, 1)]
    waiter(y_in.at[three], plane_send.at[1], plane_recv.at[1], here).wait()
    y_mid[...] = add_up(y_in).astype(BF16)
    for step in range(1, 4):
        to_x = rem(x + step, 4)
        send(y_mid.at[to_x], yx_in.at[x], plane_send.at[3], plane_recv.at[3], (to_x * 16 + z, narrow))
    yx_in[pl.ds(x, 1)] = y_mid[pl.ds(x, 1)]
    @pl.when(is_relay)
    def _():
        for piece in range(4):
            waiter(chain_in.at[piece], chain_send.at[piece], chain_recv.at[piece], here).wait_recv()
            give_pieces(piece, own_sums(piece) + add_up(chain_in.at[piece]))

    waiter(xy_in.at[three], plane_send.at[2], plane_recv.at[2], here).wait()
    waiter(yx_in.at[three], plane_send.at[3], plane_recv.at[3], here).wait()
    total = jnp.concatenate([add_up(xy_in), add_up(yx_in)], axis=0)
    rolled = pltpu.roll(total, 64, 1)
    left = iota((16, 128), 1) < 64
    for step in range(8):
        top, bottom = slice(32 * step, 32 * step + 16), slice(32 * step + 16, 32 * step + 32)
        rest = slice(256 + 8 * step, 264 + 8 * step)
        first = jnp.where(left, total[top], rolled[bottom])
        second = jnp.where(left, rolled[top], total[bottom])
        for core, packed, values in ((0, first, total), (1, second, rolled)):
            line_out[step, core] = jnp.concatenate([packed, values[rest], jnp.zeros((8, 128), F32)], axis=0).astype(BF16)

    def give_line(step, carry):
        place = rem(z + 4 + step, 8)
        to_z = 8 * c + place
        for core in range(2):
            own = jnp.logical_and(to_z == z, c == core)

            @pl.when(jnp.logical_not(own))
            def _():
                send(line_out.at[place, core], line_in.at[z], line_send, line_recv, (x * 16 + to_z, 2 * y + core))

            @pl.when(own)
            def _():
                line_in[pl.ds(z, 1)] = line_out[pl.ds(place, 1), core]

        return carry

    lax.fori_loop(0, 8, give_line, 0)

    keeps = []
    for half in range(2):
        quarters = []
        for piece in (2 * half, 2 * half + 1):
            waiter(piece_in.at[piece], chain_send.at[piece], piece_recv.at[piece], here).wait_recv()
            quarters.append(add_up(piece_in.at[piece]))
        share[half] = jnp.concatenate(quarters, axis=1).astype(BF16)
        keeps.append(pltpu.make_async_copy(share.at[half], shared.at[half, narrow], keep_sem.at[half]))
        keeps[-1].start()

        def give_share(step, carry, half=half):
            send(
                share.at[half], shared.at[half, narrow],
                share_send.at[half], share_recv.at[half], (wide, rem(narrow + step, 8)),
            )
            return carry

        lax.fori_loop(1, 8, give_share, 0)

    @pl.when(in_half == 1)
    def _():
        waiter(line_in.at[pl.ds(0, 15)], line_send, line_recv, here).wait()

    @pl.when(in_half == 0)
    def _():
        waiter(line_in, line_send, line_recv, here).wait()

    total = add_up(line_in)
    held_w[0:16] = total[0:16, 0:64]
    held_w[16:32] = total[0:16, 64:128]
    held_w[32:40] = total[16:24, 0:64]
    keeps.append(pltpu.make_async_copy(held_w, out_w, keep_sem.at[2]))
    keeps[2].start()

    waiter(asked.at[most], ask_send, ask_recv, here).wait_send()
    waiter(replies.at[most], reply_send, reply_recv, here).wait_send()

    for piece in range(4):

        @pl.when(is_source)
        def _(piece=piece):
            for step in range(4):
                waiter(shard.at[piece], shard_send.at[piece], shard_recv.at[piece], here).wait_send()

        @pl.when(passes_on)
        def _(piece=piece):
            waiter(shard.at[piece], pass_send.at[piece], shard_recv.at[piece], here).wait_send()

        waiter(chain_out.at[piece], chain_send.at[piece], chain_recv.at[piece], here).wait_send()

    for half in range(2):
        waiter(shared.at[half, pl.ds(0, 7)], share_send.at[half], share_recv.at[half], here).wait()
        keeps[half].wait()
    keeps[2].wait()


def finish_kernel(shared, sums, out_table, out_u, out_o):
    out_table[...] = shared[...].reshape(256, 256).astype(F32)
    out_u[...] = sums[0:32]
    out_o[...] = sums[32:40]


def on_device(table, item_owner, item_row, lengths, cotangent, w_uvqk, w_out):
    vmem = pl.BlockSpec(memory_space=pltpu.VMEM)
    anywhere = pl.BlockSpec(memory_space=pl.ANY)
    dma = pltpu.SemaphoreType.DMA
    shape = jax.ShapeDtypeStruct

    def held(*sizes, kind=BF16):
        return pltpu.VMEM(sizes, kind)

    shared, sums = pl.pallas_call(
        layer_kernel,
        out_shape=(shape((2, 8, 32, 256), BF16), shape((40, 64), F32)),
        in_specs=[anywhere] * 7,
        out_specs=(anywhere, anywhere),
        scratch_shapes=[
            held(1, 128, kind=I32), held(1, 128, kind=I32), held(1, 6, kind=I32),
            held(128, 512), held(512, 2048), held(512, 512),
            held(4, 256, 128), held(4, 256, 128), held(64, 8, 128, kind=F32), held(64, 8, 128, kind=F32), held(512, 256), held(512, 1024),
            held(64, 16, 256), held(64, 16, 256),
            held(128, 2048, kind=F32), held(128, 2048), held(8, 128, 128), held(8, 128, 128, kind=F32),
            held(128, 2048, kind=F32), held(128, 2048),
            held(4, 2, 320, 512), held(64, 16, 256), held(64, 16, 256),
            held(4, 320, 512), held(4, 160, 512), held(4, 4, 160, 128),
            held(4, 160, 512), held(4, 4, 160, 128), held(4, 160, 128), held(4, 160, 128),
            held(4, 160, 128), held(4, 160, 128),
            held(8, 2, 32, 128), held(16, 32, 128),
            held(2, 256, 256, kind=F32), held(4, 2, 256, 128), held(4, 256, 128), held(4, 4, 32, 128), held(2, 32, 256), held(40, 64, kind=F32),
            dma((10,)), dma((4,)), dma((4,)), dma((4,)), dma, dma, dma, dma,
            dma, dma, dma((4,)), dma((4,)), dma((4,)), dma((4,)), dma, dma,
            dma((4,)), dma((4,)), dma((4,)), dma((2,)), dma((2,)), dma((3,)),
        ],
        compiler_params=pltpu.CompilerParams(collective_id=0, has_side_effects=True, vmem_limit_bytes=VMEM_LIMIT),
        name="layer",
    )(item_owner.reshape(1, 128), item_row.reshape(1, 128), lengths, table, cotangent, w_uvqk, w_out)

    grad_table, grad_uvqk, grad_out = pl.pallas_call(
        finish_kernel,
        out_shape=(shape((256, 512), F32), shape((32, 64), F32), shape((8, 64), F32)),
        grid=(2,),
        in_specs=[
            pl.BlockSpec((1, 8, 32, 256), lambda half: (half, 0, 0, 0)),
            pl.BlockSpec((40, 64), lambda half: (0, 0)),
        ],
        out_specs=(
            pl.BlockSpec((256, 256), lambda half: (0, half)),
            pl.BlockSpec((32, 64), lambda half: (0, 0)),
            pl.BlockSpec((8, 64), lambda half: (0, 0)),
        ),
        name="finish",
    )(shared, sums)
    return grad_table, grad_uvqk.T, grad_out.T


def solution(mesh):
    in_specs = (
        P("wide", None),
        P(("wide", "narrow"), None),
        P(("wide", "narrow")),
        P(("wide", "narrow"), None),
        P(("wide", "narrow"), None),
        P(),
        P(),
    )
    out_specs = (P("wide", None), P("narrow", "wide"), P("narrow", "wide"))
    return jax.shard_map(on_device, mesh=mesh, in_specs=in_specs, out_specs=out_specs, check_vma=False)
```

```python
import jax
import jax.numpy as jnp
from jax import lax
from jax.experimental import pallas as pl
from jax.experimental.pallas import tpu as pltpu
from jax.sharding import PartitionSpec as P

HEADS = 8
EPS = 1e-05
MESH = pl.DeviceIdType.MESH
F32, BF16, I32 = jnp.float32, jnp.bfloat16, jnp.int32
VMEM_LIMIT = 63 * 1024 * 1024


def div(value, by):
    return lax.div(value, jnp.int32(by))


def rem(value, by):
    return lax.rem(value, jnp.int32(by))


def coordinates():
    wide, narrow = lax.axis_index("wide"), lax.axis_index("narrow")
    return div(wide, 16), rem(wide, 16), div(narrow, 2), rem(narrow, 2)


def shard_z(y, c, b):
    return 2 * (rem(y + 2 * b, 4) + 4 * c) + 1 - b


def holder_of(z):
    b = 1 - rem(z, 2)
    half = div(z, 2)
    y = rem(rem(half, 4) + 4 - 2 * b, 4)
    return 2 * y + div(half, 4), b


def member(step, x, y, c, a, b):
    far = (div(step, 16), rem(div(step, 4), 4))
    dx, dy = [jnp.where(i == 0, 2, jnp.where(i == 1, 1, jnp.where(i == 2, 3, 0))) for i in far]
    to_x, to_y = rem(x + dx, 4), rem(y + dy, 4)
    to_b, to_c = rem(b + 1 + rem(div(step, 2), 2), 2), rem(c + 1 + rem(step, 2), 2)
    return to_x * 16 + shard_z(to_y, to_c, to_b), (to_x * 16 + 2 * a + to_b, 2 * to_y + to_c)


def mixed_member(step, x, y, c, a, b):
    chip = div(step, 4)
    place = jnp.where(chip < 3, chip, jnp.where(chip < 15, chip + 1, 3))
    far = (rem(rem(place, 4) + div(place, 4), 4), rem(place, 4))
    dx, dy = [jnp.where(i == 0, 2, jnp.where(i == 1, 1, jnp.where(i == 2, 3, 0))) for i in far]
    to_x, to_y = rem(x + dx, 4), rem(y + dy, 4)
    to_b, to_c = rem(b + 1 + rem(div(step, 2), 2), 2), rem(c + 1 + rem(step, 2), 2)
    return to_x * 16 + shard_z(to_y, to_c, to_b), (to_x * 16 + 2 * a + to_b, 2 * to_y + to_c)


def signal(sem, device):
    pl.semaphore_signal(sem, inc=1, device_id=device, device_id_type=MESH)


def send(src, dst, send_sem, recv_sem, device):
    pltpu.make_async_remote_copy(
        src_ref=src, dst_ref=dst, send_sem=send_sem, recv_sem=recv_sem, device_id=device, device_id_type=MESH
    ).start()


def waiter(ref, send_sem, recv_sem, device):
    return pltpu.make_async_remote_copy(
        src_ref=ref, dst_ref=ref, send_sem=send_sem, recv_sem=recv_sem, device_id=device, device_id_type=MESH
    )


def iota(shape, dim):
    return lax.broadcasted_iota(I32, shape, dim)


def onehot(hits):
    return jnp.where(hits, 1.0, 0.0).astype(BF16)


def dot(left, right, contract=((1,), (0,))):
    return lax.dot_general(left, right, (contract, ((), ())), preferred_element_type=F32)


def ranks(owner_t, owner_s):
    sub, lane = iota((128, 128), 0), iota((128, 128), 1)
    same = owner_t == owner_s
    across = jnp.sum(jnp.where(same & (sub < lane), 1.0, 0.0), axis=0, keepdims=True)
    down = jnp.sum(jnp.where(same & (lane < sub), 1.0, 0.0), axis=1, keepdims=True)
    return down, across


def to_blocks(first, second, lanes):
    return jnp.concatenate([first.reshape(64, 8, lanes), second.reshape(64, 8, lanes)], axis=1).astype(BF16)


def mean_rows(values):
    return jnp.mean(values, axis=-1, keepdims=True)


def norm_back(grad, normed, scale):
    return scale * (grad - mean_rows(grad) - normed * mean_rows(grad * normed))


def weights_of_pairs(lengths):
    sub, lane = iota((128, 128), 0), iota((128, 128), 1)
    seg_t, seg_s = jnp.zeros((128, 128), I32), jnp.zeros((128, 128), I32)
    total = jnp.zeros((1, 1), I32)
    for i in range(6):
        total = total + lengths[0:1, i : i + 1]
        seg_t = seg_t + jnp.where(sub >= total, 1, 0)
        seg_s = seg_s + jnp.where(lane >= total, 1, 0)
    own_length = jnp.ones((128, 128), F32)
    for i in range(6):
        own_length = jnp.where(seg_t == i, lengths[0:1, i : i + 1].astype(F32), own_length)
    return jnp.where((seg_t == seg_s) & (lane <= sub), 1.0 / own_length, 0.0)


def layer_kernel(
    owner_hbm, row_hbm, lengths_hbm, table, cotangent_hbm, w_uvqk_hbm, w_out_hbm, shared, out_w,
    owner, row, lengths, cotangent, w_uvqk, w_out, own_shard, shard, ask_out, asked, chosen, gathers, reply_out, replies,
    slope, act, held_att, att_slope, grad_act, grad_pre, grads, rows_out, rows_in, pair_in, x_out, y_out, x_in, y_in, x_mid, y_mid, xy_in, yx_in,
    line_out, line_in, sums, chain_in, chain_out, piece_in, share, held_w,
    load_sem, shard_send, shard_recv, pass_send, ask_send, ask_recv, reply_send, reply_recv,
    rows_send, rows_recv, pair_send, pair_recv, plane_send, plane_recv, line_send, line_recv,
    chain_send, chain_recv, piece_recv, share_send, share_recv, keep_sem,
):
    x, z, y, c = coordinates()
    wide = x * 16 + z
    a, b = div(z, 2), rem(z, 2)
    narrow = 2 * y + c
    here = (wide, narrow)
    my_z = shard_z(y, c, b)
    me = x * 16 + my_z
    to_narrow, to_b = holder_of(z)
    is_source = to_narrow == narrow
    away = rem(z - my_z + 16, 16)
    outward = jnp.where(away < 8, 1, -1)
    hops = jnp.where(away < 8, away, 16 - away)
    is_relay = hops == 3
    passes_on = jnp.logical_or(hops == 3, hops == 5)
    is_far = hops > 3
    upper = div(z, 8)
    in_half = (upper == c).astype(I32)
    barrier = pltpu.get_barrier_semaphore()

    def on_line(at_z):
        return x * 16 + rem(at_z + 32, 16), narrow

    loads = []
    for i, (src, dst) in enumerate(
        [(owner_hbm, owner), (row_hbm, row), (lengths_hbm, lengths), (w_uvqk_hbm, w_uvqk), (cotangent_hbm, cotangent), (w_out_hbm, w_out)]
        + [(table.at[:, pl.ds(128 * piece, 128)], own_shard.at[piece]) for piece in range(4)]
    ):
        loads.append(pltpu.make_async_copy(src, dst, load_sem.at[i]))
        loads[-1].start()

    parent = jnp.where(hops > 3, my_z + 3 * outward, my_z)
    signal(barrier, on_line(jnp.where(hops > 3, z - 2 * outward, my_z)))

    def greet(step, carry):
        signal(barrier, member(step, x, y, c, a, b)[1])
        return carry

    lax.fori_loop(0, 63, greet, 0, unroll=7)

    loads[0].wait()
    loads[1].wait()
    owner_s = jnp.broadcast_to(owner[...].astype(F32), (128, 128))
    owner_t = owner_s.T
    rank_t, rank_s = ranks(owner_t, owner_s)
    slot_s = (owner_s * 8.0 + rank_s)[0:1].astype(I32)
    slot_t = (owner_t * 16.0 + rank_t)[:, 0:1].astype(I32)
    slots = onehot(iota((512, 128), 0) == slot_s)
    named = (jnp.broadcast_to(row[...].astype(F32), (128, 128)).T + 1.0).astype(BF16)
    ask_out[...] = dot(slots, named).reshape(64, 8, 128)

    for piece in range(4):
        loads[6 + piece].wait()
    pl.semaphore_wait(barrier, 63 + 4 * is_source.astype(I32) + passes_on.astype(I32))

    @pl.when(is_source)
    def _():
        for steps in ((3, -3), (1, -1)):
            for piece in range(4):
                for step in steps:
                    send(
                        own_shard.at[piece], shard.at[piece],
                        shard_send.at[piece], shard_recv.at[piece], on_line(z + step),
                    )

    def ask(step, carry):
        rank, device = member(step, x, y, c, a, b)
        send(ask_out.at[rank], asked.at[me], ask_send, ask_recv, device)
        return carry

    lax.fori_loop(0, 63, ask, 0, unroll=7)
    asked[pl.ds(me, 1)] = ask_out[pl.ds(me, 1)]
    most = pl.ds(0, 63)

    @pl.when(passes_on)
    def _():
        for piece in range(4):
            waiter(shard.at[piece], shard_send.at[piece], shard_recv.at[piece], here).wait_recv()
            send(
                shard.at[piece], shard.at[piece],
                pass_send.at[piece], shard_recv.at[piece], on_line(z + outward * 2),
            )

    waiter(asked.at[most], ask_send, ask_recv, here).wait_recv()
    wanted = asked[...].reshape(512, 128).astype(I32)
    wanted = jnp.concatenate([wanted, wanted], axis=1)
    chosen[...] = onehot(wanted == iota((512, 256), 1) + 1)
    @pl.when(jnp.logical_not(passes_on))
    def _():
        for piece in range(4):
            waiter(shard.at[piece], shard_send.at[piece], shard_recv.at[piece], here).wait_recv()

    first = dot(chosen[...], jnp.concatenate([shard[0], shard[1]], axis=1))
    second = dot(chosen[...], jnp.concatenate([shard[2], shard[3]], axis=1))
    reply_out[...] = to_blocks(first, second, 256)

    def answer(step, carry):
        rank, device = mixed_member(step, x, y, c, a, b)
        send(reply_out.at[rank], replies.at[me], reply_send, reply_recv, device)
        return carry

    lax.fori_loop(0, 63, answer, 0)
    replies[pl.ds(me, 1)] = reply_out[pl.ds(me, 1)]

    none = jnp.zeros((64, 8, 256), F32)
    hits = chosen[...].astype(F32).reshape(64, 8, 256)
    for half in range(2):
        spread = jnp.concatenate([none, hits] if half else [hits, none], axis=1)
        gathers[256 * half : 256 * half + 256] = spread.reshape(1024, 256).T.astype(BF16)
    loads[2].wait()
    weight = weights_of_pairs(lengths)
    spots = iota((128, 1024), 1)
    finds = (onehot(spots == slot_t), onehot(spots == slot_t + 8))
    waiter(replies.at[most], reply_send, reply_recv, here).wait_recv()
    arrived = replies[...].reshape(1024, 256)
    embedded = jnp.concatenate([dot(finds[0], arrived), dot(finds[1], arrived)], axis=1)
    center = embedded - mean_rows(embedded)
    embed_scale = lax.rsqrt(mean_rows(center * center) + EPS)
    embed_norm = center * embed_scale
    normed = embed_norm.astype(BF16)

    loads[3].wait()
    for part in range(4):
        cols = pl.ds(512 * part, 512)
        value = dot(normed, w_uvqk[:, cols])
        gain = jax.nn.sigmoid(value)
        act[:, cols] = (value * gain).astype(BF16)
        slope[:, cols] = gain * (1.0 + value * (1.0 - gain))

    first_half = iota((128, 128), 1) < 64
    keep = (first_half, jnp.logical_not(first_half))
    zero = jnp.zeros((128, 128), BF16)
    mixed = []
    for pair in range(4):
        q = act[:, 1024 + 128 * pair : 1152 + 128 * pair]
        k = act[:, 1536 + 128 * pair : 1664 + 128 * pair]
        v = act[:, 512 + 128 * pair : 640 + 128 * pair]
        both = jnp.zeros((128, 128), F32)
        for head in range(2):
            score = dot(jnp.where(keep[head], q, zero), k, ((1,), (1,))) * 0.125
            gain = jax.nn.sigmoid(score)
            attention = (score * gain * weight).astype(BF16)
            held_att[2 * pair + head] = attention
            att_slope[2 * pair + head] = weight * (gain * (1.0 + score * (1.0 - gain))) * 0.125
            both = both + dot(attention, jnp.where(keep[head], v, zero))
        mixed.append(both)
    mixture = jnp.concatenate(mixed, axis=1)
    center = mixture - mean_rows(mixture)
    mix_scale = lax.rsqrt(mean_rows(center * center) + EPS)
    mix_norm = center * mix_scale
    gate = act[:, 0:512].astype(F32)
    gated = (mix_norm * gate).astype(BF16)

    loads[4].wait()
    loads[5].wait()
    cot = cotangent[...]

    def back(part, grad_normed):
        cols = pl.ds(512 * part, 512)
        grad_pre[:, cols] = (grad_act[:, cols] * slope[:, cols]).astype(BF16)
        return grad_normed + dot(grad_pre[:, cols], w_uvqk[:, cols], ((1,), (1,)))

    grad_gated = dot(cot, w_out[...], ((1,), (1,)))
    grad_act[:, 0:512] = grad_gated * mix_norm
    grad_normed = back(0, jnp.zeros((128, 512), F32))
    grad_mix = norm_back(grad_gated * gate, mix_norm, mix_scale).astype(BF16)
    for pair in range(4):
        q = act[:, 1024 + 128 * pair : 1152 + 128 * pair]
        k = act[:, 1536 + 128 * pair : 1664 + 128 * pair]
        v = act[:, 512 + 128 * pair : 640 + 128 * pair]
        g = grad_mix[:, 128 * pair : 128 * pair + 128]
        grad_q, grad_k, grad_v = [jnp.zeros((128, 128), F32)] * 3
        for head in range(2):
            q_one, k_one, v_one, g_one = [jnp.where(keep[head], part, zero) for part in (q, k, v, g)]
            grad_att = dot(g_one, v, ((1,), (1,)))
            grad_score = (grad_att * att_slope[2 * pair + head]).astype(BF16)
            grad_v = grad_v + dot(held_att[2 * pair + head], g_one, ((0,), (0,)))
            grad_q = grad_q + dot(grad_score, k_one)
            grad_k = grad_k + dot(grad_score, q_one, ((0,), (0,)))
        grad_act[:, 512 + 128 * pair : 640 + 128 * pair] = grad_v
        grad_act[:, 1024 + 128 * pair : 1152 + 128 * pair] = grad_q
        grad_act[:, 1536 + 128 * pair : 1664 + 128 * pair] = grad_k
    for part in range(1, 4):
        grad_normed = back(part, grad_normed)
    grad_embed = (cot.astype(F32) + norm_back(grad_normed, embed_norm, embed_scale)).astype(BF16)

    given = dot(slots, grad_embed)
    rows_out[...] = to_blocks(given[:, 0:256], given[:, 256:512], 256)

    def give_rows(step, carry):
        rank, device = mixed_member(step, x, y, c, a, b)
        send(rows_out.at[rank], rows_in.at[me], rows_send, rows_recv, device)
        return carry

    lax.fori_loop(0, 63, give_rows, 0, unroll=7)
    rows_in[pl.ds(me, 1)] = rows_out[pl.ds(me, 1)]

    grad_o = dot(cot, gated, ((0,), (0,))).astype(BF16)
    partner = (wide, 2 * y + 1 - c)
    for part in range(4):
        grad_u = dot(grad_pre[:, pl.ds(512 * part, 512)], normed, ((0,), (0,))).astype(BF16)
        for side in range(2):
            grads[part, side, 0:256] = grad_u[256 * side : 256 * side + 256]
            grads[part, side, 256:320] = grad_o[128 * part + 64 * side : 128 * part + 64 * side + 64]
        send(grads.at[part, 1 - c], pair_in.at[part], pair_send.at[part], pair_recv.at[part], partner)
    for part in range(4):
        waiter(pair_in.at[part], pair_send.at[part], pair_recv.at[part], here).wait()
        both = grads[part, pl.ds(c, 1)].reshape(320, 512) + pair_in[part]
        x_out[part] = both[0:160]
        for to in range(4):
            y_out[to, part] = both[160:320, 128 * to : 128 * to + 128]
    for step in range(1, 4):
        to_x, to_y = rem(x + step, 4), rem(y + step, 4)
        send(
            x_out.at[to_x], x_in.at[x], plane_send.at[0], plane_recv.at[0],
            (to_x * 16 + z, narrow),
        )
        send(
            y_out.at[to_y], y_in.at[y],
            plane_send.at[1], plane_recv.at[1], (wide, 2 * to_y + c),
        )
    x_in[pl.ds(x, 1)] = x_out[pl.ds(x, 1)]
    y_in[pl.ds(y, 1)] = y_out[pl.ds(y, 1)]

    waiter(rows_in.at[most], rows_send, rows_recv, here).wait()
    sums[...] = dot(gathers[...], rows_in[...].reshape(1024, 256)).reshape(2, 256, 256)

    child = (hops == 7).astype(I32)
    place = jnp.where(hops == 1, 0, 1) + 1 - outward

    def give_pieces(piece, values):
        chain_out[piece] = values.astype(BF16)

        def give(step, carry):
            to = rem(narrow + step, 8)
            send(
                chain_out.at[piece, pl.ds(pl.multiple_of(32 * to, 32), 32)], piece_in.at[piece, place],
                chain_send.at[piece], piece_recv.at[piece], (x * 16 + my_z, to),
            )
            return carry

        lax.fori_loop(0, 8, give, 0)

    def own_sums(piece):
        return sums[piece // 2, :, 128 * (piece % 2) : 128 * (piece % 2) + 128]

    @pl.when(is_far)
    def _():
        for piece in range(4):
            chain_out[piece] = own_sums(piece).astype(BF16)
            send(
                chain_out.at[piece], chain_in.at[piece, child],
                chain_send.at[piece], chain_recv.at[piece], on_line(parent),
            )

    @pl.when(hops == 1)
    def _():
        for piece in range(4):
            give_pieces(piece, own_sums(piece))

    three = pl.ds(0, 3)

    def add_up(ref):
        total = ref[0].astype(F32)
        for step in range(1, ref.shape[0]):
            total = total + ref[step].astype(F32)
        return total

    waiter(x_in.at[three], plane_send.at[0], plane_recv.at[0], here).wait()
    total = add_up(x_in).astype(BF16)
    for to in range(4):
        x_mid[to] = total[:, 128 * to : 128 * to + 128]
    for step in range(1, 4):
        to_y = rem(y + step, 4)
        send(
            x_mid.at[to_y], xy_in.at[y],
            plane_send.at[2], plane_recv.at[2], (wide, 2 * to_y + c),
        )
    xy_in[pl.ds(y, 1)] = x_mid[pl.ds(y, 1)]
    waiter(y_in.at[three], plane_send.at[1], plane_recv.at[1], here).wait()
    y_mid[...] = add_up(y_in).astype(BF16)
    for step in range(1, 4):
        to_x = rem(x + step, 4)
        send(y_mid.at[to_x], yx_in.at[x], plane_send.at[3], plane_recv.at[3], (to_x * 16 + z, narrow))
    yx_in[pl.ds(x, 1)] = y_mid[pl.ds(x, 1)]
    @pl.when(is_relay)
    def _():
        for piece in range(4):
            waiter(chain_in.at[piece], chain_send.at[piece], chain_recv.at[piece], here).wait_recv()
            give_pieces(piece, own_sums(piece) + add_up(chain_in.at[piece]))

    waiter(xy_in.at[three], plane_send.at[2], plane_recv.at[2], here).wait()
    waiter(yx_in.at[three], plane_send.at[3], plane_recv.at[3], here).wait()
    total = jnp.concatenate([add_up(xy_in), add_up(yx_in)], axis=0)
    rolled = pltpu.roll(total, 64, 1)
    left = iota((16, 128), 1) < 64
    for step in range(8):
        top, bottom = slice(32 * step, 32 * step + 16), slice(32 * step + 16, 32 * step + 32)
        rest = slice(256 + 8 * step, 264 + 8 * step)
        first = jnp.where(left, total[top], rolled[bottom])
        second = jnp.where(left, rolled[top], total[bottom])
        for core, packed, values in ((0, first, total), (1, second, rolled)):
            line_out[step, core] = jnp.concatenate([packed, values[rest], jnp.zeros((8, 128), F32)], axis=0).astype(BF16)

    def give_line(step, carry):
        place = rem(z + step + 4 * in_half, 8)
        to_z = 8 * c + place
        for core in range(2):
            own = jnp.logical_and(to_z == z, c == core)

            @pl.when(jnp.logical_not(own))
            def _():
                send(line_out.at[place, core], line_in.at[z], line_send, line_recv, (x * 16 + to_z, 2 * y + core))

            @pl.when(own)
            def _():
                line_in[pl.ds(z, 1)] = line_out[pl.ds(place, 1), core]

        return carry

    lax.fori_loop(0, 8, give_line, 0)

    keeps = []
    for half in range(2):
        quarters = []
        for piece in (2 * half, 2 * half + 1):
            waiter(piece_in.at[piece], chain_send.at[piece], piece_recv.at[piece], here).wait_recv()
            quarters.append(add_up(piece_in.at[piece]))
        share[half] = jnp.concatenate(quarters, axis=1).astype(BF16)
        keeps.append(pltpu.make_async_copy(share.at[half], shared.at[half, narrow], keep_sem.at[half]))
        keeps[-1].start()

        def give_share(step, carry, half=half):
            send(
                share.at[half], shared.at[half, narrow],
                share_send.at[half], share_recv.at[half], (wide, rem(narrow + step, 8)),
            )
            return carry

        lax.fori_loop(1, 8, give_share, 0)

    @pl.when(in_half == 1)
    def _():
        waiter(line_in.at[pl.ds(0, 15)], line_send, line_recv, here).wait()

    @pl.when(in_half == 0)
    def _():
        waiter(line_in, line_send, line_recv, here).wait()

    total = add_up(line_in)
    held_w[0:16] = total[0:16, 0:64]
    held_w[16:32] = total[0:16, 64:128]
    held_w[32:40] = total[16:24, 0:64]
    keeps.append(pltpu.make_async_copy(held_w, out_w, keep_sem.at[2]))
    keeps[2].start()

    waiter(asked.at[most], ask_send, ask_recv, here).wait_send()
    waiter(replies.at[most], reply_send, reply_recv, here).wait_send()

    for piece in range(4):

        @pl.when(is_source)
        def _(piece=piece):
            for step in range(4):
                waiter(shard.at[piece], shard_send.at[piece], shard_recv.at[piece], here).wait_send()

        @pl.when(passes_on)
        def _(piece=piece):
            waiter(shard.at[piece], pass_send.at[piece], shard_recv.at[piece], here).wait_send()

        waiter(chain_out.at[piece], chain_send.at[piece], chain_recv.at[piece], here).wait_send()

    for half in range(2):
        waiter(shared.at[half, pl.ds(0, 7)], share_send.at[half], share_recv.at[half], here).wait()
        keeps[half].wait()
    keeps[2].wait()


def finish_kernel(shared, sums, out_table, out_u, out_o):
    out_table[...] = shared[...].reshape(256, 256).astype(F32)
    out_u[...] = sums[0:32]
    out_o[...] = sums[32:40]


def on_device(table, item_owner, item_row, lengths, cotangent, w_uvqk, w_out):
    vmem = pl.BlockSpec(memory_space=pltpu.VMEM)
    anywhere = pl.BlockSpec(memory_space=pl.ANY)
    dma = pltpu.SemaphoreType.DMA
    shape = jax.ShapeDtypeStruct

    def held(*sizes, kind=BF16):
        return pltpu.VMEM(sizes, kind)

    shared, sums = pl.pallas_call(
        layer_kernel,
        out_shape=(shape((2, 8, 32, 256), BF16), shape((40, 64), F32)),
        in_specs=[anywhere] * 7,
        out_specs=(anywhere, anywhere),
        scratch_shapes=[
            held(1, 128, kind=I32), held(1, 128, kind=I32), held(1, 6, kind=I32),
            held(128, 512), held(512, 2048), held(512, 512),
            held(4, 256, 128), held(4, 256, 128), held(64, 8, 128, kind=F32), held(64, 8, 128, kind=F32), held(512, 256), held(512, 1024),
            held(64, 16, 256), held(64, 16, 256),
            held(128, 2048, kind=F32), held(128, 2048), held(8, 128, 128), held(8, 128, 128, kind=F32),
            held(128, 2048, kind=F32), held(128, 2048),
            held(4, 2, 320, 512), held(64, 16, 256), held(64, 16, 256),
            held(4, 320, 512), held(4, 160, 512), held(4, 4, 160, 128),
            held(4, 160, 512), held(4, 4, 160, 128), held(4, 160, 128), held(4, 160, 128),
            held(4, 160, 128), held(4, 160, 128),
            held(8, 2, 32, 128), held(16, 32, 128),
            held(2, 256, 256, kind=F32), held(4, 2, 256, 128), held(4, 256, 128), held(4, 4, 32, 128), held(2, 32, 256), held(40, 64, kind=F32),
            dma((10,)), dma((4,)), dma((4,)), dma((4,)), dma, dma, dma, dma,
            dma, dma, dma((4,)), dma((4,)), dma((4,)), dma((4,)), dma, dma,
            dma((4,)), dma((4,)), dma((4,)), dma((2,)), dma((2,)), dma((3,)),
        ],
        compiler_params=pltpu.CompilerParams(collective_id=0, has_side_effects=True, vmem_limit_bytes=VMEM_LIMIT),
        name="layer",
    )(item_owner.reshape(1, 128), item_row.reshape(1, 128), lengths, table, cotangent, w_uvqk, w_out)

    grad_table, grad_uvqk, grad_out = pl.pallas_call(
        finish_kernel,
        out_shape=(shape((256, 512), F32), shape((32, 64), F32), shape((8, 64), F32)),
        grid=(2,),
        in_specs=[
            pl.BlockSpec((1, 8, 32, 256), lambda half: (half, 0, 0, 0)),
            pl.BlockSpec((40, 64), lambda half: (0, 0)),
        ],
        out_specs=(
            pl.BlockSpec((256, 256), lambda half: (0, half)),
            pl.BlockSpec((32, 64), lambda half: (0, 0)),
            pl.BlockSpec((8, 64), lambda half: (0, 0)),
        ),
        name="finish",
    )(shared, sums)
    return grad_table, grad_uvqk.T, grad_out.T


def solution(mesh):
    in_specs = (
        P("wide", None),
        P(("wide", "narrow"), None),
        P(("wide", "narrow")),
        P(("wide", "narrow"), None),
        P(("wide", "narrow"), None),
        P(),
        P(),
    )
    out_specs = (P("wide", None), P("narrow", "wide"), P("narrow", "wide"))
    return jax.shard_map(on_device, mesh=mesh, in_specs=in_specs, out_specs=out_specs, check_vma=False)
```
